32 devices in a mesh: groups: 2 (over y), vocab: 4 (over z), tokens: 2 (over x), pair: 2 (over core).
Axes of the slice: x: 2, y: 2, z: 4, core: 2. Of those that a mesh axis runs over, the one named last changes fastest.
Arguments:
- hidden: bfloat16 [512, 5120], P(('groups', 'tokens'), 'pair'), parts along dimension 0, may hold values from -70 to 70
- student_head_weight: bfloat16 [5120, 5120], P('pair', ('vocab', 'tokens')), may hold values from -0.25 to 0.25
- down_weight: bfloat16 [2, 5120, 64], P('tokens', 'pair'), may hold values from -0.078125 to 0.078125
- up_weight: bfloat16 [2, 64, 5120], P(None, None, ('vocab', 'tokens')), may hold values from -0.75 to 0.75
- teacher: bfloat16 [512, 5120], P(('groups', 'pair'), ('vocab', 'tokens')), parts along dimension 0, may hold values from -25 to 260
- tenant: int32 [512], P('groups'), parts along dimension 0, may hold values from 0 to 1, as said below
- counted_row_mask: int32 [512], P(('groups', 'pair')), parts along dimension 0, may hold values 0 or 1
Outputs:
- token_kl: float32 [512], P(('groups', 'pair')), parts along dimension 0
- hidden_gradient: bfloat16 [512, 5120], P(('groups', 'vocab', 'tokens'), 'pair'), parts along dimension 0
- down_gradient: bfloat16 [4, 5120, 64], P(('groups', 'tokens'), 'pair'), parts along dimension 0
- up_gradient: bfloat16 [4, 64, 5120], P('groups', None, ('vocab', 'tokens')), parts along dimension 0
The draws below stay inside these ranges and needn't reach their ends.
There are 2 independent parts, one for each index of `groups`. The reference program is written for one: setup_inputs(seed, part) draws one part's arguments, and reference() takes and returns one part's arrays. A program takes and returns all parts, laid end to end along the dimension named above; an argument that names none is the same for every part. Nothing has to cross between parts.
Inputs may be any that keep to these rules, and one draw needn't show every extreme that they name: Constant on aligned blocks of 64 rows; every tenant owns at least one block.
All inputs are finite; a program needn't handle non-finite values. No bound on the sum of `counted_row_mask` on one device may be relied on, other than what follows from the above.
Results may differ from the reference program's by a relative error of at most 0.009.
Values may be sent and summed in bfloat16 or wider, within the bound.
A program may use at most 64 MiB of HBM per device.

```python
import jax
import jax.numpy as jnp
from jax import lax

MODEL_WIDTH = 5120
ADAPTER_RANK = 64
TOKEN_ROWS = 256
BLOCK = 64
TENANT_TOTAL = 2
VOCAB_ENTRIES = 5120


def draw_hidden(key, part):
    key = jax.random.fold_in(key, 5)
    key_base = jax.random.fold_in(key, 0)
    return jnp.clip(jax.random.normal(key_base, (TOKEN_ROWS, MODEL_WIDTH), jnp.float32), -6.0, 6.0).astype(jnp.bfloat16)


def draw_teacher(key, part):
    key = jax.random.fold_in(key, 7)
    key_list = jax.random.split(key, 1)
    positions = jnp.arange(VOCAB_ENTRIES)[None, :]
    ramp = 1.1 * positions.astype(jnp.float32) / VOCAB_ENTRIES
    values = jnp.clip(3.0 * jax.random.normal(key_list[0], (TOKEN_ROWS, VOCAB_ENTRIES), jnp.float32), -12.0, 12.0)
    return (values + ramp).astype(jnp.bfloat16)


def draw_tenant(key, part):
    key = jax.random.fold_in(key, 11)
    key_order = jax.random.fold_in(key, 101)
    key_label = jax.random.fold_in(key, 202)
    key_extra = jax.random.fold_in(key, 303)
    block_count = TOKEN_ROWS // BLOCK
    order_score = jax.random.randint(key_order, (block_count,), 0, 1 << 20) * block_count + jnp.arange(block_count, dtype=jnp.int32)
    block_rank = jnp.argsort(jnp.argsort(order_score, stable=True), stable=True).astype(jnp.int32)
    label_score = jax.random.randint(key_label, (TENANT_TOTAL,), 0, 1 << 20) * TENANT_TOTAL + jnp.arange(TENANT_TOTAL, dtype=jnp.int32)
    labels = jnp.argsort(label_score, stable=True).astype(jnp.int32)
    extra = jax.random.randint(key_extra, (block_count,), 0, TENANT_TOTAL).astype(jnp.int32)
    forced = labels[jnp.minimum(block_rank, TENANT_TOTAL - 1)]
    per_block = jnp.where(block_rank < TENANT_TOTAL, forced, extra).astype(jnp.int32)
    return jnp.repeat(per_block, BLOCK).astype(jnp.int32)


def place_ends(drawn, stream_key, least, top_value):
    dims = drawn.shape
    place = [jax.random.randint(jax.random.fold_in(stream_key, axis), (), 0, dims[axis]) for axis in range(len(dims))]
    drawn = drawn.at[tuple(place)].set(least)
    longest = dims.index(max(dims))
    place[longest] = (place[longest] + 1) % dims[longest]
    return drawn.at[tuple(place)].set(top_value)


def shard_levels(own_key, shape, cuts, low, top_value):
    gain, own = 1.0, jax.random.fold_in(own_key, 6)
    for position, shards_of in cuts:
        heights = jnp.exp(jax.random.uniform(jax.random.fold_in(own, position), (shards_of,), jnp.float32, low / len(cuts), top_value / len(cuts)))
        gain = gain * jnp.repeat(heights, shape[position] // shards_of).reshape([-1 if axis == position else 1 for axis in range(len(shape))])
    return gain


def scatter_about(stream_key, dims, deviation, limit, pieces=(), kind=jnp.bfloat16):
    array = jax.random.normal(stream_key, dims, jnp.float32) * deviation
    if len(pieces) > 0:
        array = shard_levels(stream_key, dims, pieces, -0.22, 0.18) * array
    return jnp.clip(array, min=-limit, max=limit).astype(kind)


def setup_inputs(seed: int = 0, part: int = 0) -> dict:
    seeds = jax.random.split(jax.random.key(seed), 8)
    part_splits = jax.random.split(jax.random.fold_in(seeds[7], part), 8)
    hidden = draw_hidden(jax.random.fold_in(jax.random.fold_in(seeds[7], part), 71), part)
    student_head_weight = scatter_about(seeds[1], (MODEL_WIDTH, VOCAB_ENTRIES), (MODEL_WIDTH // 9) ** -0.5, 0.25, ((0, 2), (1, 8)))
    down_weight = scatter_about(seeds[2], (TENANT_TOTAL, MODEL_WIDTH, ADAPTER_RANK), MODEL_WIDTH ** -0.5, 0.078125, ((0, 2), (1, 2)))
    up_weight = scatter_about(seeds[3], (TENANT_TOTAL, ADAPTER_RANK, VOCAB_ENTRIES), ADAPTER_RANK ** -0.5, 0.75, ((2, 8),))
    teacher = draw_teacher(jax.random.fold_in(jax.random.fold_in(seeds[7], part), 71), part)
    tenant = draw_tenant(jax.random.fold_in(jax.random.fold_in(seeds[7], part), 71), part)
    counted_row_mask = place_ends((jax.random.randint(part_splits[6], (TOKEN_ROWS,), 0, 4) < 3).astype(jnp.int32), jax.random.fold_in(part_splits[6], 1), 0, 1)
    return {"hidden": hidden, "student_head_weight": student_head_weight, "down_weight": down_weight, "up_weight": up_weight, "teacher": teacher, "tenant": tenant, "counted_row_mask": counted_row_mask}


ADAPTER_SCALE = 0.5


def reference(hidden, student_head_weight, down_weight, up_weight, teacher, tenant, counted_row_mask):
    block_count = TOKEN_ROWS // BLOCK
    tenant_per_block = tenant.reshape(block_count, BLOCK)[:, 0]
    hidden_block_rows = hidden.reshape(block_count, BLOCK, MODEL_WIDTH).astype(jnp.float32)
    selected_down = down_weight[tenant_per_block].astype(jnp.float32)
    adapter_codes = jnp.einsum("nmw,nwz->nmz", hidden_block_rows, selected_down, precision=lax.Precision.HIGHEST).astype(jnp.bfloat16)
    base_output = jnp.dot(hidden, student_head_weight, preferred_element_type=jnp.float32)
    selected_up = up_weight[tenant_per_block].astype(jnp.float32)
    adapter_logits = jnp.einsum("gji,giu->gju", adapter_codes.astype(jnp.float32), selected_up, precision=lax.Precision.HIGHEST).reshape(TOKEN_ROWS, VOCAB_ENTRIES)
    student_model = base_output + ADAPTER_SCALE * adapter_logits
    teacher_logits = teacher.astype(jnp.float32)
    peak_s = jnp.max(student_model, axis=1)
    sum_s = jnp.sum(jnp.exp(student_model - peak_s[:, None]), axis=1)
    peak_t = jnp.max(teacher_logits, axis=1)
    exp_t = jnp.exp(teacher_logits - peak_t[:, None])
    sum_t = jnp.sum(exp_t, axis=1)
    cross_sum = jnp.sum(exp_t * (teacher_logits - student_model), axis=1)
    log_zs = peak_s + jnp.log(sum_s)
    log_zt = peak_t + jnp.log(sum_t)
    token_kl = cross_sum / sum_t - log_zt + log_zs
    weights = counted_row_mask.astype(jnp.float32) / TOKEN_ROWS
    loss_gradient = (weights[:, None] * (jnp.exp(student_model - log_zs[:, None]) - jnp.exp(teacher_logits - log_zt[:, None]))).astype(jnp.bfloat16)
    grad_blocks = loss_gradient.reshape(block_count, BLOCK, VOCAB_ENTRIES).astype(jnp.float32)
    code_gradient = jnp.einsum("bkv,brv->bkr", grad_blocks, selected_up, precision=lax.Precision.HIGHEST).astype(jnp.bfloat16)
    adapter_backward = jnp.einsum("xil,xvl->xiv", code_gradient.astype(jnp.float32), selected_down, precision=lax.Precision.HIGHEST).reshape(TOKEN_ROWS, MODEL_WIDTH)
    hidden_gradient = (jnp.dot(loss_gradient, student_head_weight.T, preferred_element_type=jnp.float32) + ADAPTER_SCALE * adapter_backward).astype(jnp.bfloat16)
    tenant_onehot = (tenant_per_block[:, None] == jnp.arange(TENANT_TOTAL)[None, :]).astype(jnp.float32)
    up_outer_product = jnp.einsum("bkr,bkv->brv", adapter_codes.astype(jnp.float32), grad_blocks, precision=lax.Precision.HIGHEST)
    up_gradient = (ADAPTER_SCALE * jnp.einsum("yf,ysk->fsk", tenant_onehot, up_outer_product, precision=lax.Precision.HIGHEST)).astype(jnp.bfloat16)
    down_outer_product = jnp.einsum("pht,phs->pts", hidden_block_rows, code_gradient.astype(jnp.float32), precision=lax.Precision.HIGHEST)
    down_gradient = (ADAPTER_SCALE * jnp.einsum("mi,mhe->ihe", tenant_onehot, down_outer_product, precision=lax.Precision.HIGHEST)).astype(jnp.bfloat16)
    return (token_kl, hidden_gradient, down_gradient, up_gradient)
```

```python
import functools

import jax
import jax.numpy as jnp
from jax import lax
from jax.experimental import pallas as pl
from jax.experimental.pallas import tpu as pltpu
from jax.sharding import PartitionSpec as P

BLOCK = 64


ADAPTER_SCALE = 0.5


def shards(hidden, student_head_weight, down_weight, up_weight, teacher, tenant, counted_row_mask):
    all_rows = tenant.shape[0]
    half_rows = all_rows // lax.axis_size("pair")
    pair_index = lax.axis_index("pair")
    block_count = all_rows // BLOCK
    half_blocks = half_rows // BLOCK
    tenant_per_block = tenant.reshape(block_count, BLOCK)[:, 0]
    gathered = lax.all_gather(hidden, "tokens", axis=0, tiled=True)
    width = gathered.shape[1]
    adapter_rank = down_weight.shape[2]
    columns = student_head_weight.shape[1]
    tenant_number = up_weight.shape[0]
    owner_mask = tenant == lax.axis_index("tokens")
    lookup_tables = lax.all_gather(down_weight, "tokens", axis=0, tiled=True)
    selected_down = lookup_tables[tenant_per_block]
    partial_codes = jnp.einsum(
        "nmw,nwz->nmz",
        gathered.reshape(block_count, BLOCK, width),
        selected_down,
        preferred_element_type=jnp.float32,
    ).reshape(all_rows, adapter_rank)
    summed_codes = lax.psum(partial_codes, "pair")
    adapter_codes = summed_codes.astype(jnp.bfloat16)
    slab = gathered
    trunk_logits = lax.psum_scatter(
        jnp.dot(slab, student_head_weight, preferred_element_type=jnp.float32),
        "pair",
        scatter_dimension=0,
        tiled=True,
    )
    my_codes = lax.dynamic_slice_in_dim(adapter_codes, pair_index * half_rows, half_rows, 0)
    local_tenant = lax.dynamic_slice_in_dim(
        tenant_per_block, pair_index * half_blocks, half_blocks, 0
    )
    adapter_logits = jnp.einsum(
        "gji,giu->gju",
        my_codes.reshape(half_blocks, BLOCK, adapter_rank),
        up_weight[local_tenant],
        preferred_element_type=jnp.float32,
    ).reshape(half_rows, columns)
    student_model = trunk_logits + ADAPTER_SCALE * adapter_logits
    teacher_logits = teacher.astype(jnp.float32)
    peak_s, peak_t = lax.pmax(
        (jnp.max(student_model, axis=1), jnp.max(teacher_logits, axis=1)), ("vocab", "tokens")
    )
    exp_t = jnp.exp(teacher_logits - peak_t[:, None])
    sum_s, sum_t, cross_sum = lax.psum(
        (
            jnp.sum(jnp.exp(student_model - peak_s[:, None]), axis=1),
            jnp.sum(exp_t, axis=1),
            jnp.sum(exp_t * (teacher_logits - student_model), axis=1),
        ),
        ("vocab", "tokens"),
    )
    log_zs = peak_s + jnp.log(sum_s)
    log_zt = peak_t + jnp.log(sum_t)
    token_kl = cross_sum / sum_t - log_zt + log_zs
    weights = counted_row_mask.astype(jnp.float32) / all_rows
    grad_half = (
        weights[:, None]
        * (jnp.exp(student_model - log_zs[:, None]) - jnp.exp(teacher_logits - log_zt[:, None]))
    ).astype(jnp.bfloat16)
    full_grad = lax.all_gather(grad_half, "pair", axis=0, tiled=True)
    grad_blocks = full_grad.reshape(block_count, BLOCK, columns)
    selected_up = up_weight[tenant_per_block]
    code_part = jnp.einsum(
        "bkv,brv->bkr", grad_blocks, selected_up, preferred_element_type=jnp.float32
    ).reshape(all_rows, adapter_rank)
    code_gradient = lax.psum(code_part, ("vocab", "tokens")).astype(jnp.bfloat16)
    up_outer_product = jnp.einsum(
        "bkr,bkv->brv",
        adapter_codes.reshape(block_count, BLOCK, adapter_rank),
        grad_blocks,
        preferred_element_type=jnp.float32,
    )
    tenant_onehot = (tenant_per_block[:, None] == jnp.arange(tenant_number)[None, :]).astype(
        jnp.float32
    )
    up_gradient = (
        ADAPTER_SCALE
        * jnp.einsum(
            "yf,ysk->fsk", tenant_onehot, up_outer_product, precision=lax.Precision.HIGHEST
        )
    ).astype(jnp.bfloat16)
    owned_grad = jnp.where(owner_mask[:, None], code_gradient, jnp.zeros_like(code_gradient))
    down_gradient = (
        ADAPTER_SCALE
        * jnp.einsum("kd,kr->dr", gathered, owned_grad, preferred_element_type=jnp.float32)
    )[None].astype(jnp.bfloat16)
    shard_rows = all_rows // lax.axis_size(("vocab", "tokens"))
    slab = full_grad
    total = jnp.einsum("kv,dv->kd", slab, student_head_weight, preferred_element_type=jnp.float32)
    width_gradients = lax.psum_scatter(total, ("vocab", "tokens"), scatter_dimension=0, tiled=True)
    row_start = lax.axis_index(("vocab", "tokens")) * shard_rows
    my_grad_codes = lax.dynamic_slice_in_dim(code_gradient, row_start, shard_rows, 0)
    my_row_tenant = lax.dynamic_slice_in_dim(tenant, row_start, shard_rows, 0)
    width_gradients = width_gradients + ADAPTER_SCALE * jnp.einsum(
        "kr,kdr->kd",
        my_grad_codes,
        lookup_tables[my_row_tenant],
        preferred_element_type=jnp.float32,
    )
    hidden_gradient = width_gradients.astype(jnp.bfloat16)
    return (token_kl, hidden_gradient, down_gradient, up_gradient)


F32 = jnp.float32
BF16 = jnp.bfloat16
PARTS = 5
NT = (((1,), (1,)), ((), ()))
NN = (((1,), (0,)), ((), ()))


def mm(a, b, dims=NN):
    return lax.dot_general(a, b, dims, preferred_element_type=F32)


def remote(src, dst, send, recv, where):
    return pltpu.make_async_remote_copy(
        src_ref=src, dst_ref=dst, send_sem=send, recv_sem=recv,
        device_id=where, device_id_type=pl.DeviceIdType.MESH,
    )


def fused(
    vocab_size, token_size,
    hidden, weight, down_t, up, teacher, mask, counted,
    kl_out, hidden_out, down_out, up_out,
    h, w, d_dup, d_all, up_v, teach, acc, acc_in,
    code_part, code_in, codes_mine, codes_other, codes_t,
    stats, stats_in, flip, grad, cgp, cgp_in, cg_all, cg_t,
    xs, xr, own, zs, zr,
    lsem, hs, hr, pair_s, pair_r, tok_s, tok_r,
    st_s, st_r, cp_s, cp_r, cg_s, cg_r, xs_s, xs_r, z_s, z_r,
):
    v, t, p = lax.axis_index("vocab"), lax.axis_index("tokens"), lax.axis_index("pair")
    peers = vocab_size * token_size
    me = v * token_size + t
    mate = {"pair": 1 - p}
    across = {"tokens": 1 - t}
    rows, rank2 = mask.shape
    half = rows // 2
    rank = rank2 // 2
    columns = weight.shape[1]
    width = weight.shape[0]
    part = width // PARTS
    block = rows // peers

    def peer(k):
        b = lax.rem(me + k, peers)
        return b, {"vocab": b // token_size, "tokens": lax.rem(b, token_size)}

    def at_rows(i, n):
        return pl.ds(pl.multiple_of(i * n, n), n)

    local = [
        pltpu.make_async_copy(hidden, h.at[at_rows(t, half)], lsem.at[0]),
        pltpu.make_async_copy(weight, w, lsem.at[1]),
        pltpu.make_async_copy(down_t, d_dup.at[pl.ds(0, rank)], lsem.at[2]),
        pltpu.make_async_copy(down_t, d_dup.at[pl.ds(rank, rank)], lsem.at[3]),
        pltpu.make_async_copy(down_t, d_all.at[at_rows(t, rank)], lsem.at[4]),
        pltpu.make_async_copy(up, up_v, lsem.at[5]),
        pltpu.make_async_copy(teacher, teach, lsem.at[6]),
    ]
    for copy in local:
        copy.start()

    barrier = pltpu.get_barrier_semaphore()
    pl.semaphore_signal(barrier, inc=1, device_id=mate, device_id_type=pl.DeviceIdType.MESH)
    for k in range(1, peers):
        pl.semaphore_signal(barrier, inc=1, device_id=peer(k)[1], device_id_type=pl.DeviceIdType.MESH)
    pl.semaphore_wait(barrier, peers)

    quarter = half // 2
    sends = []
    for c in range(2):
        sends.append(remote(
            hidden.at[pl.ds(c * quarter, quarter)],
            h.at[pl.ds(pl.multiple_of(t * half + c * quarter, quarter), quarter)],
            hs.at[c], hr.at[c], across,
        ))
        sends[-1].start()
    for copy in local:
        copy.wait()

    own_lane = (lax.broadcasted_iota(jnp.int32, (1, rank2), 1) // rank == t).astype(F32)

    def forward(start, n):
        sl = pl.ds(pl.multiple_of(start, n), n)
        piece = h[sl, :]
        code_part[sl, :] = mm(piece, d_dup[...], NT) * mask[sl, :] * own_lane
        return sl, piece

    sl, piece = forward(t * half, half)
    acc[sl, :] = mm(piece, w[...])
    for c in range(2):
        sends[c].wait_recv()
        sl, piece = forward((1 - t) * half + c * quarter, quarter)
        if c == 1:
            code_pair = remote(code_part, code_in, pair_s.at[0], pair_r.at[0], mate)
            code_pair.start()
        acc[sl, :] = mm(piece, w[...])
    mate_rows = at_rows(1 - p, half)
    my_rows = at_rows(p, half)
    logit_pair = remote(acc.at[mate_rows], acc_in, pair_s.at[1], pair_r.at[1], mate)
    logit_pair.start()
    code_pair.wait_recv()
    codes_mine[...] = (code_part[...] + code_in[...]).astype(BF16)
    code_tok = remote(codes_mine, codes_other, tok_s.at[0], tok_r.at[0], across)
    code_tok.start()

    tl = teach[...].astype(F32)
    peak_t = jnp.max(tl, axis=1, keepdims=True)
    exp_t = jnp.exp(tl - peak_t)
    sum_t = jnp.sum(exp_t, axis=1, keepdims=True)

    logit_pair.wait_recv()
    code_tok.wait_recv()
    down_tok = remote(d_dup.at[pl.ds(0, rank)], d_all.at[at_rows(t, rank)], tok_s.at[1], tok_r.at[1], across)
    codes = (codes_mine[...].astype(F32) + codes_other[...].astype(F32))
    codes_mine_half = (codes_mine[my_rows, :].astype(F32) + codes_other[my_rows, :].astype(F32)).astype(BF16)
    student = acc[my_rows, :] + acc_in[...] + ADAPTER_SCALE * mm(codes_mine_half, up_v[...])
    peak_s = jnp.max(student, axis=1, keepdims=True)
    sum_s = jnp.sum(jnp.exp(student - peak_s), axis=1, keepdims=True)
    cross = jnp.sum(exp_t * (tl - student), axis=1, keepdims=True)

    lane = lax.broadcasted_iota(jnp.int32, (half, 128), 1)
    packed = jnp.zeros((half, 128), F32)
    for i, value in enumerate((peak_s, sum_s, peak_t, sum_t, cross)):
        packed = jnp.where(lane == i, value, packed)
    stats[...] = packed.T[:8, :]
    stat_sends = []
    for k in range(1, peers):
        stat_sends.append(remote(stats, stats_in.at[me], st_s.at[k], st_r.at[k], peer(k)[1]))
        stat_sends[-1].start()
    down_tok.start()
    stats_in[me] = stats[...]
    codes_t[...] = codes.T.astype(BF16)
    for copy in stat_sends:
        copy.wait_recv()
    got = [stats_in[i] for i in range(peers)]
    top_s, top_t = got[0][0:1], got[0][2:3]
    for one in got[1:]:
        top_s, top_t = jnp.maximum(top_s, one[0:1]), jnp.maximum(top_t, one[2:3])
    zs_sum = zt_sum = cross_sum = jnp.zeros_like(top_s)
    for one in got:
        zs_sum = zs_sum + one[1:2] * jnp.exp(one[0:1] - top_s)
        scale = jnp.exp(one[2:3] - top_t)
        zt_sum = zt_sum + one[3:4] * scale
        cross_sum = cross_sum + one[4:5] * scale
    log_zs = top_s + jnp.log(zs_sum)
    log_zt = top_t + jnp.log(zt_sum)
    kl_out[...] = cross_sum / zt_sum - log_zt + log_zs
    flip[...] = jnp.zeros_like(flip)
    flip[0:1, :] = log_zs
    flip[1:2, :] = log_zt
    flip[2:3, :] = counted[...].astype(F32) / rows
    cols = flip[...].T
    grad_half = (cols[:, 2:3] * (jnp.exp(student - cols[:, 0:1]) - jnp.exp(tl - cols[:, 1:2]))).astype(BF16)
    vh = vocab_size // 2
    my_blocks = pl.ds(p * vh, vh)
    grad[my_blocks] = grad_half.reshape(vh, token_size, block, columns)
    grad_pair = remote(grad.at[my_blocks], grad.at[my_blocks], pair_s.at[2], pair_r.at[2], mate)
    grad_pair.start()
    grad_pair.wait_recv()

    group = vocab_size * block
    g_other = grad[:, 1 - t].reshape(group, columns)
    x_sends = []
    for j in range(PARTS):
        xs[j] = mm(g_other, w[pl.ds(j * part, part), :], NT).astype(BF16).reshape(vocab_size, block, part)
        x_sends.append(remote(xs.at[j], xr.at[j], xs_s.at[j], xs_r.at[j], across))
        x_sends[-1].start()
        if j == 0:
            g_all = grad[...].reshape(rows, columns)
            cgp[...] = (mm(g_all, up_v[...], NT) * mask[...]).astype(BF16).reshape(peers, block, rank2)
            cp_sends = []
            for k in range(1, peers):
                b, where = peer(k)
                cp_sends.append(remote(cgp.at[b], cgp_in.at[me], cp_s.at[k], cp_r.at[k], where))
                cp_sends[-1].start()
            cgp_in[me] = cgp[me]
    g_own = grad[:, t].reshape(group, columns)
    for j in range(PARTS):
        own[j] = mm(g_own, w[pl.ds(j * part, part), :], NT).reshape(vocab_size, block, part)

    for copy in cp_sends:
        copy.wait_recv()
    total = cgp_in[0].astype(F32)
    for i in range(1, peers):
        total = total + cgp_in[i].astype(F32)
    cg_all[me] = total.astype(BF16)
    cg_sends = []
    for k in range(1, peers):
        cg_sends.append(remote(cg_all.at[me], cg_all.at[me], cg_s.at[k], cg_r.at[k], peer(k)[1]))
        cg_sends[-1].start()

    up_out[...] = (ADAPTER_SCALE * mm(codes_t[...], g_all)).astype(BF16)

    z_sends = []
    for j in range(PARTS):
        x_sends[j].wait_recv()
        merged = own[j] + xr[j].astype(F32)
        own[j] = merged
        zs[j] = merged.astype(BF16)
        for k in range(1, vocab_size):
            to = lax.rem(v + k, vocab_size)
            z_sends.append(remote(zs.at[j, to], zr.at[j, k], z_s.at[j, k], z_r.at[j, k], {"vocab": to}))
            z_sends[-1].start()
        if j == 0:
            for copy in cg_sends:
                copy.wait_recv()
            cg_t[...] = cg_all[...].reshape(rows, rank2).astype(F32).T.astype(BF16)
            mine = cg_t[at_rows(t, rank), :]
        down_out[:, pl.ds(j * part, part)] = (ADAPTER_SCALE * mm(mine, h[:, pl.ds(j * part, part)])).astype(BF16)

    down_tok.wait_recv()
    my_cg = cg_all[me]
    for j in range(PARTS):
        for k in range(1, vocab_size):
            z_sends[j * (vocab_size - 1) + k - 1].wait_recv()
        value = own[j, v] + ADAPTER_SCALE * mm(my_cg, d_all[:, pl.ds(j * part, part)])
        for k in range(1, vocab_size):
            value = value + zr[j, k].astype(F32)
        hidden_out[:, pl.ds(j * part, part)] = value.astype(BF16)

    for copy in [code_pair, logit_pair, grad_pair, code_tok, down_tok] + sends + stat_sends + cp_sends + cg_sends + x_sends + z_sends:
        copy.wait_send()


def fused_shards(hidden, student_head_weight, down_weight, up_weight, teacher, tenant, counted_row_mask):
    vocab_size, token_size = lax.axis_size("vocab"), lax.axis_size("tokens")
    peers = vocab_size * token_size
    rows = tenant.shape[0]
    half = rows // 2
    block = rows // peers
    width, columns = student_head_weight.shape
    tenants, rank, _ = up_weight.shape
    rank2 = tenants * rank
    part = width // PARTS
    mask = (tenant[:, None] == (jnp.arange(rank2) // rank)[None, :]).astype(F32)
    down_t = jnp.swapaxes(down_weight[0], 0, 1)
    vmem = pl.BlockSpec(memory_space=pltpu.VMEM)
    hbm = pl.BlockSpec(memory_space=pl.ANY)
    dma = pltpu.SemaphoreType.DMA
    kernel = functools.partial(fused, vocab_size, token_size)
    token_kl, hidden_gradient, down_gradient, up_gradient = pl.pallas_call(
        kernel,
        out_shape=(
            jax.ShapeDtypeStruct((1, half), F32),
            jax.ShapeDtypeStruct((block, width), BF16),
            jax.ShapeDtypeStruct((rank, width), BF16),
            jax.ShapeDtypeStruct((rank2, columns), BF16),
        ),
        in_specs=[hbm] * 5 + [vmem] * 2,
        out_specs=(vmem,) * 4,
        scratch_shapes=[
            pltpu.VMEM((rows, width), BF16),
            pltpu.VMEM((width, columns), BF16),
            pltpu.VMEM((rank2, width), BF16),
            pltpu.VMEM((rank2, width), BF16),
            pltpu.VMEM((rank2, columns), BF16),
            pltpu.VMEM((half, columns), BF16),
            pltpu.VMEM((rows, columns), F32),
            pltpu.VMEM((half, columns), F32),
            pltpu.VMEM((rows, rank2), F32),
            pltpu.VMEM((rows, rank2), F32),
            pltpu.VMEM((rows, rank2), BF16),
            pltpu.VMEM((rows, rank2), BF16),
            pltpu.VMEM((rank2, rows), BF16),
            pltpu.VMEM((8, half), F32),
            pltpu.VMEM((peers, 8, half), F32),
            pltpu.VMEM((128, half), F32),
            pltpu.VMEM((vocab_size, token_size, block, columns), BF16),
            pltpu.VMEM((peers, block, rank2), BF16),
            pltpu.VMEM((peers, block, rank2), BF16),
            pltpu.VMEM((peers, block, rank2), BF16),
            pltpu.VMEM((rank2, rows), BF16),
            pltpu.VMEM((PARTS, vocab_size, block, part), BF16),
            pltpu.VMEM((PARTS, vocab_size, block, part), BF16),
            pltpu.VMEM((PARTS, vocab_size, block, part), F32),
            pltpu.VMEM((PARTS, vocab_size, block, part), BF16),
            pltpu.VMEM((PARTS, vocab_size, block, part), BF16),
            dma((7,)), dma((2,)), dma((2,)), dma((3,)), dma((3,)), dma((2,)), dma((2,)),
            dma((peers,)), dma((peers,)), dma((peers,)), dma((peers,)), dma((peers,)), dma((peers,)),
            dma((PARTS,)), dma((PARTS,)), dma((PARTS, vocab_size)), dma((PARTS, vocab_size)),
        ],
        compiler_params=pltpu.CompilerParams(
            collective_id=0, has_side_effects=True, vmem_limit_bytes=40 << 20
        ),
    )(hidden, student_head_weight, down_t, up_weight.reshape(rank2, columns), teacher, mask,
      counted_row_mask.reshape(1, half))
    return (
        token_kl.reshape(half),
        hidden_gradient,
        jnp.swapaxes(down_gradient, 0, 1)[None],
        up_gradient.reshape(tenants, rank, columns),
    )


def fits(mesh):
    return mesh.shape["tokens"] == 2 and mesh.shape["vocab"] == 4


def solution(mesh):
    return jax.shard_map(
        fused_shards if fits(mesh) else shards,
        mesh=mesh,
        in_specs=(
            P(("groups", "tokens"), "pair"),
            P("pair", ("vocab", "tokens")),
            P("tokens", "pair", None),
            P(None, None, ("vocab", "tokens")),
            P(("groups", "pair"), ("vocab", "tokens")),
            P("groups"),
            P(("groups", "pair")),
        ),
        out_specs=(
            P(("groups", "pair")),
            P(("groups", "vocab", "tokens"), "pair"),
            P(("groups", "tokens"), "pair", None),
            P("groups", None, ("vocab", "tokens")),
        ),
        check_vma=False,
    )
```

```python
import functools

import jax
import jax.numpy as jnp
from jax import lax
from jax.experimental import pallas as pl
from jax.experimental.pallas import tpu as pltpu
from jax.sharding import PartitionSpec as P

BLOCK = 64


ADAPTER_SCALE = 0.5


def shards(hidden, student_head_weight, down_weight, up_weight, teacher, tenant, counted_row_mask):
    all_rows = tenant.shape[0]
    half_rows = all_rows // lax.axis_size("pair")
    pair_index = lax.axis_index("pair")
    block_count = all_rows // BLOCK
    half_blocks = half_rows // BLOCK
    tenant_per_block = tenant.reshape(block_count, BLOCK)[:, 0]
    gathered = lax.all_gather(hidden, "tokens", axis=0, tiled=True)
    width = gathered.shape[1]
    adapter_rank = down_weight.shape[2]
    columns = student_head_weight.shape[1]
    tenant_number = up_weight.shape[0]
    owner_mask = tenant == lax.axis_index("tokens")
    lookup_tables = lax.all_gather(down_weight, "tokens", axis=0, tiled=True)
    selected_down = lookup_tables[tenant_per_block]
    partial_codes = jnp.einsum(
        "nmw,nwz->nmz",
        gathered.reshape(block_count, BLOCK, width),
        selected_down,
        preferred_element_type=jnp.float32,
    ).reshape(all_rows, adapter_rank)
    summed_codes = lax.psum(partial_codes, "pair")
    adapter_codes = summed_codes.astype(jnp.bfloat16)
    slab = gathered
    trunk_logits = lax.psum_scatter(
        jnp.dot(slab, student_head_weight, preferred_element_type=jnp.float32),
        "pair",
        scatter_dimension=0,
        tiled=True,
    )
    my_codes = lax.dynamic_slice_in_dim(adapter_codes, pair_index * half_rows, half_rows, 0)
    local_tenant = lax.dynamic_slice_in_dim(
        tenant_per_block, pair_index * half_blocks, half_blocks, 0
    )
    adapter_logits = jnp.einsum(
        "gji,giu->gju",
        my_codes.reshape(half_blocks, BLOCK, adapter_rank),
        up_weight[local_tenant],
        preferred_element_type=jnp.float32,
    ).reshape(half_rows, columns)
    student_model = trunk_logits + ADAPTER_SCALE * adapter_logits
    teacher_logits = teacher.astype(jnp.float32)
    peak_s, peak_t = lax.pmax(
        (jnp.max(student_model, axis=1), jnp.max(teacher_logits, axis=1)), ("vocab", "tokens")
    )
    exp_t = jnp.exp(teacher_logits - peak_t[:, None])
    sum_s, sum_t, cross_sum = lax.psum(
        (
            jnp.sum(jnp.exp(student_model - peak_s[:, None]), axis=1),
            jnp.sum(exp_t, axis=1),
            jnp.sum(exp_t * (teacher_logits - student_model), axis=1),
        ),
        ("vocab", "tokens"),
    )
    log_zs = peak_s + jnp.log(sum_s)
    log_zt = peak_t + jnp.log(sum_t)
    token_kl = cross_sum / sum_t - log_zt + log_zs
    weights = counted_row_mask.astype(jnp.float32) / all_rows
    grad_half = (
        weights[:, None]
        * (jnp.exp(student_model - log_zs[:, None]) - jnp.exp(teacher_logits - log_zt[:, None]))
    ).astype(jnp.bfloat16)
    full_grad = lax.all_gather(grad_half, "pair", axis=0, tiled=True)
    grad_blocks = full_grad.reshape(block_count, BLOCK, columns)
    selected_up = up_weight[tenant_per_block]
    code_part = jnp.einsum(
        "bkv,brv->bkr", grad_blocks, selected_up, preferred_element_type=jnp.float32
    ).reshape(all_rows, adapter_rank)
    code_gradient = lax.psum(code_part, ("vocab", "tokens")).astype(jnp.bfloat16)
    up_outer_product = jnp.einsum(
        "bkr,bkv->brv",
        adapter_codes.reshape(block_count, BLOCK, adapter_rank),
        grad_blocks,
        preferred_element_type=jnp.float32,
    )
    tenant_onehot = (tenant_per_block[:, None] == jnp.arange(tenant_number)[None, :]).astype(
        jnp.float32
    )
    up_gradient = (
        ADAPTER_SCALE
        * jnp.einsum(
            "yf,ysk->fsk", tenant_onehot, up_outer_product, precision=lax.Precision.HIGHEST
        )
    ).astype(jnp.bfloat16)
    owned_grad = jnp.where(owner_mask[:, None], code_gradient, jnp.zeros_like(code_gradient))
    down_gradient = (
        ADAPTER_SCALE
        * jnp.einsum("kd,kr->dr", gathered, owned_grad, preferred_element_type=jnp.float32)
    )[None].astype(jnp.bfloat16)
    shard_rows = all_rows // lax.axis_size(("vocab", "tokens"))
    slab = full_grad
    total = jnp.einsum("kv,dv->kd", slab, student_head_weight, preferred_element_type=jnp.float32)
    width_gradients = lax.psum_scatter(total, ("vocab", "tokens"), scatter_dimension=0, tiled=True)
    row_start = lax.axis_index(("vocab", "tokens")) * shard_rows
    my_grad_codes = lax.dynamic_slice_in_dim(code_gradient, row_start, shard_rows, 0)
    my_row_tenant = lax.dynamic_slice_in_dim(tenant, row_start, shard_rows, 0)
    width_gradients = width_gradients + ADAPTER_SCALE * jnp.einsum(
        "kr,kdr->kd",
        my_grad_codes,
        lookup_tables[my_row_tenant],
        preferred_element_type=jnp.float32,
    )
    hidden_gradient = width_gradients.astype(jnp.bfloat16)
    return (token_kl, hidden_gradient, down_gradient, up_gradient)


F32 = jnp.float32
BF16 = jnp.bfloat16
PARTS = 10
PIECES = 4
NT = (((1,), (1,)), ((), ()))
NN = (((1,), (0,)), ((), ()))


def mm(a, b, dims=NN):
    return lax.dot_general(a, b, dims, preferred_element_type=F32)


def remote(src, dst, send, recv, where):
    return pltpu.make_async_remote_copy(
        src_ref=src, dst_ref=dst, send_sem=send, recv_sem=recv,
        device_id=where, device_id_type=pl.DeviceIdType.MESH,
    )


def fused(
    vocab_size, token_size,
    hidden, weight, down_t, up, teacher, mask, counted,
    kl_out, hidden_out, down_out, up_out,
    h, w, d_dup, d_all, up_v, teach, acc, acc_in,
    code_part, code_in, codes_mine, codes_other, codes_t,
    stats, stats_in, flip, grad, cgp, cgp_in, cg_all, cg_t,
    xs, xr, own, zs, zr,
    lsem, hs, hr, fs, fr, pair_s, pair_r, tok_s, tok_r,
    st_s, st_r, cp_s, cp_r, cg_s, cg_r, dn_s, dn_r, xs_s, xs_r, z_s, z_r,
):
    v, t, p = lax.axis_index("vocab"), lax.axis_index("tokens"), lax.axis_index("pair")
    peers = vocab_size * token_size
    me = v * token_size + t
    mate = {"pair": 1 - p}
    across = {"tokens": 1 - t}
    rows, rank2 = mask.shape
    half = rows // 2
    rank = rank2 // 2
    columns = weight.shape[1]
    width = weight.shape[0]
    part = width // PARTS
    block = rows // peers

    def peer(k):
        b = lax.rem(me + k, peers)
        return b, {"vocab": b // token_size, "tokens": lax.rem(b, token_size)}

    def at_rows(i, n):
        return pl.ds(pl.multiple_of(i * n, n), n)

    local = [
        pltpu.make_async_copy(hidden, h.at[at_rows(t, half)], lsem.at[0]),
        pltpu.make_async_copy(weight, w, lsem.at[1]),
        pltpu.make_async_copy(down_t, d_dup.at[pl.ds(0, rank)], lsem.at[2]),
        pltpu.make_async_copy(down_t, d_dup.at[pl.ds(rank, rank)], lsem.at[3]),
        pltpu.make_async_copy(down_t, d_all.at[at_rows(t, rank)], lsem.at[4]),
        pltpu.make_async_copy(up, up_v, lsem.at[5]),
        pltpu.make_async_copy(teacher, teach, lsem.at[6]),
    ]
    for copy in local:
        copy.start()

    barrier = pltpu.get_barrier_semaphore()
    pl.semaphore_signal(barrier, inc=1, device_id=mate, device_id_type=pl.DeviceIdType.MESH)
    for k in range(1, peers):
        pl.semaphore_signal(barrier, inc=1, device_id=peer(k)[1], device_id_type=pl.DeviceIdType.MESH)
    pl.semaphore_wait(barrier, peers)

    quarter = half // 2
    piece_rows = quarter // PIECES
    odd = lax.rem(v, 2)
    neighbour = {"vocab": v + 1 - 2 * odd}
    sends, forwards = [], []
    for c in range(PIECES):
        start = odd * quarter + c * piece_rows
        sends.append(remote(
            hidden.at[pl.ds(pl.multiple_of(start, piece_rows), piece_rows)],
            h.at[pl.ds(pl.multiple_of(t * half + start, piece_rows), piece_rows)],
            hs.at[c], hr.at[c], across,
        ))
        sends[-1].start()
    for copy in local:
        copy.wait()

    own_lane = (lax.broadcasted_iota(jnp.int32, (1, rank2), 1) // rank == t).astype(F32)

    def forward(start, n):
        sl = pl.ds(pl.multiple_of(start, n), n)
        piece = h[sl, :]
        code_part[sl, :] = mm(piece, d_dup[...], NT) * mask[sl, :] * own_lane
        return sl, piece

    sl, piece = forward(t * half, half)
    acc[sl, :] = mm(piece, w[...])
    for c in range(PIECES):
        sends[c].wait_recv()
        start = pl.multiple_of((1 - t) * half + odd * quarter + c * piece_rows, piece_rows)
        there = h.at[pl.ds(start, piece_rows)]
        forwards.append(remote(there, there, fs.at[c], fr.at[c], neighbour))
        forwards[-1].start()
    sl, piece = forward((1 - t) * half + odd * quarter, quarter)
    acc[sl, :] = mm(piece, w[...])
    for copy in forwards:
        copy.wait_recv()
    sl, piece = forward((1 - t) * half + (1 - odd) * quarter, quarter)
    code_pair = remote(code_part, code_in, pair_s.at[0], pair_r.at[0], mate)
    code_pair.start()
    acc[sl, :] = mm(piece, w[...])
    mate_rows = at_rows(1 - p, half)
    my_rows = at_rows(p, half)
    logit_pair = remote(acc.at[mate_rows], acc_in, pair_s.at[1], pair_r.at[1], mate)
    logit_pair.start()
    code_pair.wait_recv()
    codes_mine[...] = (code_part[...] + code_in[...]).astype(BF16)
    code_tok = remote(codes_mine, codes_other, tok_s.at[0], tok_r.at[0], across)
    code_tok.start()
    share = rank // vocab_size
    sent = pl.ds(pl.multiple_of(t * rank + v * share, share), share)
    down_tok = remote(d_dup.at[at_rows(v, share)], d_all.at[sent], tok_s.at[1], tok_r.at[1], across)
    down_tok.start()

    tl = teach[...].astype(F32)
    peak_t = jnp.max(tl, axis=1, keepdims=True)
    exp_t = jnp.exp(tl - peak_t)
    sum_t = jnp.sum(exp_t, axis=1, keepdims=True)

    logit_pair.wait_recv()
    code_tok.wait_recv()
    codes = (codes_mine[...].astype(F32) + codes_other[...].astype(F32))
    codes_mine_half = (codes_mine[my_rows, :].astype(F32) + codes_other[my_rows, :].astype(F32)).astype(BF16)
    student = acc[my_rows, :] + acc_in[...] + ADAPTER_SCALE * mm(codes_mine_half, up_v[...])
    peak_s = jnp.max(student, axis=1, keepdims=True)
    sum_s = jnp.sum(jnp.exp(student - peak_s), axis=1, keepdims=True)
    cross = jnp.sum(exp_t * (tl - student), axis=1, keepdims=True)

    lane = lax.broadcasted_iota(jnp.int32, (half, 128), 1)
    packed = jnp.zeros((half, 128), F32)
    for i, value in enumerate((peak_s, sum_s, peak_t, sum_t, cross)):
        packed = jnp.where(lane == i, value, packed)
    stats[...] = packed.T[:8, :]
    stat_sends = []
    for k in range(1, peers):
        stat_sends.append(remote(stats, stats_in.at[me], st_s.at[k], st_r.at[k], peer(k)[1]))
        stat_sends[-1].start()
    stats_in[me] = stats[...]
    codes_t[...] = codes.T.astype(BF16)
    for copy in stat_sends:
        copy.wait_recv()
    got = [stats_in[i] for i in range(peers)]
    top_s, top_t = got[0][0:1], got[0][2:3]
    for one in got[1:]:
        top_s, top_t = jnp.maximum(top_s, one[0:1]), jnp.maximum(top_t, one[2:3])
    zs_sum = zt_sum = cross_sum = jnp.zeros_like(top_s)
    for one in got:
        zs_sum = zs_sum + one[1:2] * jnp.exp(one[0:1] - top_s)
        scale = jnp.exp(one[2:3] - top_t)
        zt_sum = zt_sum + one[3:4] * scale
        cross_sum = cross_sum + one[4:5] * scale
    log_zs = top_s + jnp.log(zs_sum)
    log_zt = top_t + jnp.log(zt_sum)
    kl_out[...] = cross_sum / zt_sum - log_zt + log_zs
    flip[...] = jnp.zeros_like(flip)
    flip[0:1, :] = log_zs
    flip[1:2, :] = log_zt
    flip[2:3, :] = counted[...].astype(F32) / rows
    cols = flip[...].T
    grad_half = (cols[:, 2:3] * (jnp.exp(student - cols[:, 0:1]) - jnp.exp(tl - cols[:, 1:2]))).astype(BF16)
    vh = vocab_size // 2
    my_blocks = pl.ds(p * vh, vh)
    grad[my_blocks] = grad_half.reshape(vh, token_size, block, columns)
    grad_pair = remote(grad.at[my_blocks], grad.at[my_blocks], pair_s.at[2], pair_r.at[2], mate)
    grad_pair.start()
    down_tok.wait_recv()
    arrived = d_all.at[pl.ds(pl.multiple_of((1 - t) * rank + v * share, share), share)]
    down_sends = []
    for k in range(1, vocab_size):
        down_sends.append(remote(arrived, arrived, dn_s.at[k], dn_r.at[k], {"vocab": lax.rem(v + k, vocab_size)}))
        down_sends[-1].start()
    grad_pair.wait_recv()

    group = vocab_size * block
    g_other = grad[:, 1 - t].reshape(group, columns)
    x_sends = []
    for j in range(PARTS):
        xs[j] = mm(g_other, w[pl.ds(j * part, part), :], NT).astype(BF16).reshape(vocab_size, block, part)
        x_sends.append(remote(xs.at[j], xr.at[j], xs_s.at[j], xs_r.at[j], across))
        x_sends[-1].start()
        if j == 0:
            g_all = grad[...].reshape(rows, columns)
            cgp[...] = (mm(g_all, up_v[...], NT) * mask[...]).astype(BF16).reshape(peers, block, rank2)
            cp_sends = []
            for k in range(1, peers):
                b, where = peer(k)
                cp_sends.append(remote(cgp.at[b], cgp_in.at[me], cp_s.at[k], cp_r.at[k], where))
                cp_sends[-1].start()
            cgp_in[me] = cgp[me]
    g_own = grad[:, t].reshape(group, columns)
    for j in range(PARTS):
        own[j] = mm(g_own, w[pl.ds(j * part, part), :], NT).reshape(vocab_size, block, part)

    up_out[...] = (ADAPTER_SCALE * mm(codes_t[...], g_all)).astype(BF16)

    z_sends = []
    for j in range(PARTS):
        if j == PARTS // 2:
            for copy in cp_sends:
                copy.wait_recv()
            total = cgp_in[0].astype(F32)
            for i in range(1, peers):
                total = total + cgp_in[i].astype(F32)
            cg_all[me] = total.astype(BF16)
            cg_sends = []
            for k in range(1, peers):
                cg_sends.append(remote(cg_all.at[me], cg_all.at[me], cg_s.at[k], cg_r.at[k], peer(k)[1]))
                cg_sends[-1].start()
        x_sends[j].wait_recv()
        merged = own[j] + xr[j].astype(F32)
        own[j] = merged
        zs[j] = merged.astype(BF16)
        for k in range(1, vocab_size):
            to = lax.rem(v + k, vocab_size)
            z_sends.append(remote(zs.at[j, to], zr.at[j, k], z_s.at[j, k], z_r.at[j, k], {"vocab": to}))
            z_sends[-1].start()
    for copy in cg_sends:
        copy.wait_recv()
    cg_t[...] = cg_all[...].reshape(rows, rank2).astype(F32).T.astype(BF16)
    down_out[...] = (ADAPTER_SCALE * mm(cg_t[at_rows(t, rank), :], h[...])).astype(BF16)

    for copy in down_sends:
        copy.wait_recv()
    my_cg = cg_all[me]
    for j in range(PARTS):
        for k in range(1, vocab_size):
            z_sends[j * (vocab_size - 1) + k - 1].wait_recv()
        value = own[j, v] + ADAPTER_SCALE * mm(my_cg, d_all[:, pl.ds(j * part, part)])
        for k in range(1, vocab_size):
            value = value + zr[j, k].astype(F32)
        hidden_out[:, pl.ds(j * part, part)] = value.astype(BF16)

    for copy in [code_pair, logit_pair, grad_pair, code_tok, down_tok] + sends + forwards + down_sends + stat_sends + cp_sends + cg_sends + x_sends + z_sends:
        copy.wait_send()


def fused_shards(hidden, student_head_weight, down_weight, up_weight, teacher, tenant, counted_row_mask):
    vocab_size, token_size = lax.axis_size("vocab"), lax.axis_size("tokens")
    peers = vocab_size * token_size
    rows = tenant.shape[0]
    half = rows // 2
    block = rows // peers
    width, columns = student_head_weight.shape
    tenants, rank, _ = up_weight.shape
    rank2 = tenants * rank
    part = width // PARTS
    mask = (tenant[:, None] == (jnp.arange(rank2) // rank)[None, :]).astype(F32)
    down_t = jnp.swapaxes(down_weight[0], 0, 1)
    vmem = pl.BlockSpec(memory_space=pltpu.VMEM)
    hbm = pl.BlockSpec(memory_space=pl.ANY)
    dma = pltpu.SemaphoreType.DMA
    kernel = functools.partial(fused, vocab_size, token_size)
    token_kl, hidden_gradient, down_gradient, up_gradient = pl.pallas_call(
        kernel,
        out_shape=(
            jax.ShapeDtypeStruct((1, half), F32),
            jax.ShapeDtypeStruct((block, width), BF16),
            jax.ShapeDtypeStruct((rank, width), BF16),
            jax.ShapeDtypeStruct((rank2, columns), BF16),
        ),
        in_specs=[hbm] * 5 + [vmem] * 2,
        out_specs=(vmem,) * 4,
        scratch_shapes=[
            pltpu.VMEM((rows, width), BF16),
            pltpu.VMEM((width, columns), BF16),
            pltpu.VMEM((rank2, width), BF16),
            pltpu.VMEM((rank2, width), BF16),
            pltpu.VMEM((rank2, columns), BF16),
            pltpu.VMEM((half, columns), BF16),
            pltpu.VMEM((rows, columns), F32),
            pltpu.VMEM((half, columns), F32),
            pltpu.VMEM((rows, rank2), F32),
            pltpu.VMEM((rows, rank2), F32),
            pltpu.VMEM((rows, rank2), BF16),
            pltpu.VMEM((rows, rank2), BF16),
            pltpu.VMEM((rank2, rows), BF16),
            pltpu.VMEM((8, half), F32),
            pltpu.VMEM((peers, 8, half), F32),
            pltpu.VMEM((128, half), F32),
            pltpu.VMEM((vocab_size, token_size, block, columns), BF16),
            pltpu.VMEM((peers, block, rank2), BF16),
            pltpu.VMEM((peers, block, rank2), BF16),
            pltpu.VMEM((peers, block, rank2), BF16),
            pltpu.VMEM((rank2, rows), BF16),
            pltpu.VMEM((PARTS, vocab_size, block, part), BF16),
            pltpu.VMEM((PARTS, vocab_size, block, part), BF16),
            pltpu.VMEM((PARTS, vocab_size, block, part), F32),
            pltpu.VMEM((PARTS, vocab_size, block, part), BF16),
            pltpu.VMEM((PARTS, vocab_size, block, part), BF16),
            dma((7,)), dma((PIECES,)), dma((PIECES,)), dma((PIECES,)), dma((PIECES,)), dma((3,)), dma((3,)), dma((2,)), dma((2,)),
            dma((peers,)), dma((peers,)), dma((peers,)), dma((peers,)), dma((peers,)), dma((peers,)),
            dma((vocab_size,)), dma((vocab_size,)), dma((PARTS,)), dma((PARTS,)), dma((PARTS, vocab_size)), dma((PARTS, vocab_size)),
        ],
        compiler_params=pltpu.CompilerParams(
            collective_id=0, has_side_effects=True, vmem_limit_bytes=60 << 20
        ),
    )(hidden, student_head_weight, down_t, up_weight.reshape(rank2, columns), teacher, mask,
      counted_row_mask.reshape(1, half))
    return (
        token_kl.reshape(half),
        hidden_gradient,
        jnp.swapaxes(down_gradient, 0, 1)[None],
        up_gradient.reshape(tenants, rank, columns),
    )


def fits(mesh):
    return mesh.shape["tokens"] == 2 and mesh.shape["vocab"] == 4


def solution(mesh):
    return jax.shard_map(
        fused_shards if fits(mesh) else shards,
        mesh=mesh,
        in_specs=(
            P(("groups", "tokens"), "pair"),
            P("pair", ("vocab", "tokens")),
            P("tokens", "pair", None),
            P(None, None, ("vocab", "tokens")),
            P(("groups", "pair"), ("vocab", "tokens")),
            P("groups"),
            P(("groups", "pair")),
        ),
        out_specs=(
            P(("groups", "pair")),
            P(("groups", "vocab", "tokens"), "pair"),
            P(("groups", "tokens"), "pair", None),
            P("groups", None, ("vocab", "tokens")),
        ),
        check_vma=False,
    )
```

```python
import functools

import jax
import jax.numpy as jnp
from jax import lax
from jax.experimental import pallas as pl
from jax.experimental.pallas import tpu as pltpu
from jax.sharding import PartitionSpec as P

BLOCK = 64


ADAPTER_SCALE = 0.5


def shards(hidden, student_head_weight, down_weight, up_weight, teacher, tenant, counted_row_mask):
    all_rows = tenant.shape[0]
    half_rows = all_rows // lax.axis_size("pair")
    pair_index = lax.axis_index("pair")
    block_count = all_rows // BLOCK
    half_blocks = half_rows // BLOCK
    tenant_per_block = tenant.reshape(block_count, BLOCK)[:, 0]
    gathered = lax.all_gather(hidden, "tokens", axis=0, tiled=True)
    width = gathered.shape[1]
    adapter_rank = down_weight.shape[2]
    columns = student_head_weight.shape[1]
    tenant_number = up_weight.shape[0]
    owner_mask = tenant == lax.axis_index("tokens")
    lookup_tables = lax.all_gather(down_weight, "tokens", axis=0, tiled=True)
    selected_down = lookup_tables[tenant_per_block]
    partial_codes = jnp.einsum(
        "nmw,nwz->nmz",
        gathered.reshape(block_count, BLOCK, width),
        selected_down,
        preferred_element_type=jnp.float32,
    ).reshape(all_rows, adapter_rank)
    summed_codes = lax.psum(partial_codes, "pair")
    adapter_codes = summed_codes.astype(jnp.bfloat16)
    slab = gathered
    trunk_logits = lax.psum_scatter(
        jnp.dot(slab, student_head_weight, preferred_element_type=jnp.float32),
        "pair",
        scatter_dimension=0,
        tiled=True,
    )
    my_codes = lax.dynamic_slice_in_dim(adapter_codes, pair_index * half_rows, half_rows, 0)
    local_tenant = lax.dynamic_slice_in_dim(
        tenant_per_block, pair_index * half_blocks, half_blocks, 0
    )
    adapter_logits = jnp.einsum(
        "gji,giu->gju",
        my_codes.reshape(half_blocks, BLOCK, adapter_rank),
        up_weight[local_tenant],
        preferred_element_type=jnp.float32,
    ).reshape(half_rows, columns)
    student_model = trunk_logits + ADAPTER_SCALE * adapter_logits
    teacher_logits = teacher.astype(jnp.float32)
    peak_s, peak_t = lax.pmax(
        (jnp.max(student_model, axis=1), jnp.max(teacher_logits, axis=1)), ("vocab", "tokens")
    )
    exp_t = jnp.exp(teacher_logits - peak_t[:, None])
    sum_s, sum_t, cross_sum = lax.psum(
        (
            jnp.sum(jnp.exp(student_model - peak_s[:, None]), axis=1),
            jnp.sum(exp_t, axis=1),
            jnp.sum(exp_t * (teacher_logits - student_model), axis=1),
        ),
        ("vocab", "tokens"),
    )
    log_zs = peak_s + jnp.log(sum_s)
    log_zt = peak_t + jnp.log(sum_t)
    token_kl = cross_sum / sum_t - log_zt + log_zs
    weights = counted_row_mask.astype(jnp.float32) / all_rows
    grad_half = (
        weights[:, None]
        * (jnp.exp(student_model - log_zs[:, None]) - jnp.exp(teacher_logits - log_zt[:, None]))
    ).astype(jnp.bfloat16)
    full_grad = lax.all_gather(grad_half, "pair", axis=0, tiled=True)
    grad_blocks = full_grad.reshape(block_count, BLOCK, columns)
    selected_up = up_weight[tenant_per_block]
    code_part = jnp.einsum(
        "bkv,brv->bkr", grad_blocks, selected_up, preferred_element_type=jnp.float32
    ).reshape(all_rows, adapter_rank)
    code_gradient = lax.psum(code_part, ("vocab", "tokens")).astype(jnp.bfloat16)
    up_outer_product = jnp.einsum(
        "bkr,bkv->brv",
        adapter_codes.reshape(block_count, BLOCK, adapter_rank),
        grad_blocks,
        preferred_element_type=jnp.float32,
    )
    tenant_onehot = (tenant_per_block[:, None] == jnp.arange(tenant_number)[None, :]).astype(
        jnp.float32
    )
    up_gradient = (
        ADAPTER_SCALE
        * jnp.einsum(
            "yf,ysk->fsk", tenant_onehot, up_outer_product, precision=lax.Precision.HIGHEST
        )
    ).astype(jnp.bfloat16)
    owned_grad = jnp.where(owner_mask[:, None], code_gradient, jnp.zeros_like(code_gradient))
    down_gradient = (
        ADAPTER_SCALE
        * jnp.einsum("kd,kr->dr", gathered, owned_grad, preferred_element_type=jnp.float32)
    )[None].astype(jnp.bfloat16)
    shard_rows = all_rows // lax.axis_size(("vocab", "tokens"))
    slab = full_grad
    total = jnp.einsum("kv,dv->kd", slab, student_head_weight, preferred_element_type=jnp.float32)
    width_gradients = lax.psum_scatter(total, ("vocab", "tokens"), scatter_dimension=0, tiled=True)
    row_start = lax.axis_index(("vocab", "tokens")) * shard_rows
    my_grad_codes = lax.dynamic_slice_in_dim(code_gradient, row_start, shard_rows, 0)
    my_row_tenant = lax.dynamic_slice_in_dim(tenant, row_start, shard_rows, 0)
    width_gradients = width_gradients + ADAPTER_SCALE * jnp.einsum(
        "kr,kdr->kd",
        my_grad_codes,
        lookup_tables[my_row_tenant],
        preferred_element_type=jnp.float32,
    )
    hidden_gradient = width_gradients.astype(jnp.bfloat16)
    return (token_kl, hidden_gradient, down_gradient, up_gradient)


F32 = jnp.float32
BF16 = jnp.bfloat16
PARTS = 10
PIECES = 4
NT = (((1,), (1,)), ((), ()))
NN = (((1,), (0,)), ((), ()))


def mm(a, b, dims=NN):
    return lax.dot_general(a, b, dims, preferred_element_type=F32)


def remote(src, dst, send, recv, where):
    return pltpu.make_async_remote_copy(
        src_ref=src, dst_ref=dst, send_sem=send, recv_sem=recv,
        device_id=where, device_id_type=pl.DeviceIdType.MESH,
    )


def fused(
    vocab_size, token_size,
    hidden, weight, down_t, up, teacher, tenant, counted,
    kl_out, hidden_out, down_out, up_out,
    mask, h, w, d_dup, d_all, up_v, teach, acc, acc_in,
    code_part, code_in, codes_mine, codes_other, codes_t,
    stats, stats_in, flip, grad, cgp, cgp_in, cg_all, cg_t,
    xs, xr, own, zs, zr,
    lsem, hs, hr, fs, fr, pair_s, pair_r, tok_s, tok_r,
    st_s, st_r, cp_s, cp_r, cg_s, cg_r, dn_s, dn_r, xs_s, xs_r, z_s, z_r,
):
    v, t, p = lax.axis_index("vocab"), lax.axis_index("tokens"), lax.axis_index("pair")
    peers = vocab_size * token_size
    me = v * token_size + t
    mate = {"pair": 1 - p}
    across = {"tokens": 1 - t}
    rows, rank2 = mask.shape
    half = rows // 2
    rank = rank2 // 2
    columns = weight.shape[1]
    width = weight.shape[0]
    part = width // PARTS
    block = rows // peers

    def peer(k):
        b = lax.rem(me + k, peers)
        return b, {"vocab": b // token_size, "tokens": lax.rem(b, token_size)}

    def at_rows(i, n):
        return pl.ds(pl.multiple_of(i * n, n), n)

    local = [
        pltpu.make_async_copy(hidden, h.at[at_rows(t, half)], lsem.at[0]),
        pltpu.make_async_copy(weight, w, lsem.at[1]),
        pltpu.make_async_copy(down_t, d_dup.at[pl.ds(0, rank)], lsem.at[2]),
        pltpu.make_async_copy(down_t, d_dup.at[pl.ds(rank, rank)], lsem.at[3]),
        pltpu.make_async_copy(down_t, d_all.at[at_rows(t, rank)], lsem.at[4]),
        pltpu.make_async_copy(up, up_v, lsem.at[5]),
        pltpu.make_async_copy(teacher, teach, lsem.at[6]),
    ]
    for copy in local:
        copy.start()

    barrier = pltpu.get_barrier_semaphore()
    pl.semaphore_signal(barrier, inc=1, device_id=mate, device_id_type=pl.DeviceIdType.MESH)
    for k in range(1, peers):
        pl.semaphore_signal(barrier, inc=1, device_id=peer(k)[1], device_id_type=pl.DeviceIdType.MESH)
    pl.semaphore_wait(barrier, peers)

    quarter = half // 2
    piece_rows = quarter // PIECES
    odd = lax.rem(v, 2)
    neighbour = {"vocab": v + 1 - 2 * odd}
    sends, forwards = [], []
    for c in range(PIECES):
        start = odd * quarter + c * piece_rows
        sends.append(remote(
            hidden.at[pl.ds(pl.multiple_of(start, piece_rows), piece_rows)],
            h.at[pl.ds(pl.multiple_of(t * half + start, piece_rows), piece_rows)],
            hs.at[c], hr.at[c], across,
        ))
        sends[-1].start()

    tenant_of = lax.broadcasted_iota(jnp.int32, (rank2, rows), 0) // rank
    mask[...] = (tenant_of == tenant[...]).astype(F32).T

    for copy in local:
        copy.wait()

    own_lane = (lax.broadcasted_iota(jnp.int32, (1, rank2), 1) // rank == t).astype(F32)

    def forward(start, n):
        sl = pl.ds(pl.multiple_of(start, n), n)
        piece = h[sl, :]
        code_part[sl, :] = mm(piece, d_dup[...], NT) * mask[sl, :] * own_lane
        return sl, piece

    sl, piece = forward(t * half, half)
    acc[sl, :] = mm(piece, w[...])
    for c in range(PIECES):
        sends[c].wait_recv()
        start = pl.multiple_of((1 - t) * half + odd * quarter + c * piece_rows, piece_rows)
        there = h.at[pl.ds(start, piece_rows)]
        forwards.append(remote(there, there, fs.at[c], fr.at[c], neighbour))
        forwards[-1].start()
    sl, piece = forward((1 - t) * half + odd * quarter, quarter)
    acc[sl, :] = mm(piece, w[...])
    for copy in forwards:
        copy.wait_recv()
    sl, piece = forward((1 - t) * half + (1 - odd) * quarter, quarter)
    code_pair = remote(code_part, code_in, pair_s.at[0], pair_r.at[0], mate)
    code_pair.start()
    acc[sl, :] = mm(piece, w[...])
    mate_rows = at_rows(1 - p, half)
    my_rows = at_rows(p, half)
    logit_pair = remote(acc.at[mate_rows], acc_in, pair_s.at[1], pair_r.at[1], mate)
    logit_pair.start()
    code_pair.wait_recv()
    codes_mine[...] = (code_part[...] + code_in[...]).astype(BF16)
    code_tok = remote(codes_mine.at[my_rows], codes_other.at[my_rows], tok_s.at[0], tok_r.at[0], across)
    code_tok.start()
    code_rest = remote(codes_mine.at[mate_rows], codes_other.at[mate_rows], tok_s.at[2], tok_r.at[2], across)
    code_rest.start()
    share = rank // vocab_size
    sent = pl.ds(pl.multiple_of(t * rank + v * share, share), share)
    down_tok = remote(d_dup.at[at_rows(v, share)], d_all.at[sent], tok_s.at[1], tok_r.at[1], across)
    down_tok.start()

    tl = teach[...].astype(F32)
    peak_t = jnp.max(tl, axis=1, keepdims=True)
    exp_t = jnp.exp(tl - peak_t)
    sum_t = jnp.sum(exp_t, axis=1, keepdims=True)

    logit_pair.wait_recv()
    code_tok.wait_recv()
    codes_mine_half = (codes_mine[my_rows, :].astype(F32) + codes_other[my_rows, :].astype(F32)).astype(BF16)
    student = acc[my_rows, :] + acc_in[...] + ADAPTER_SCALE * mm(codes_mine_half, up_v[...])
    peak_s = jnp.max(student, axis=1, keepdims=True)
    sum_s = jnp.sum(jnp.exp(student - peak_s), axis=1, keepdims=True)
    cross = jnp.sum(exp_t * (tl - student), axis=1, keepdims=True)

    lane = lax.broadcasted_iota(jnp.int32, (half, 128), 1)
    packed = jnp.zeros((half, 128), F32)
    for i, value in enumerate((peak_s, sum_s, peak_t, sum_t, cross)):
        packed = jnp.where(lane == i, value, packed)
    stats[...] = packed.T[:8, :]
    stat_sends = []
    for k in range(1, peers):
        stat_sends.append(remote(stats, stats_in.at[me], st_s.at[k], st_r.at[k], peer(k)[1]))
        stat_sends[-1].start()
    stats_in[me] = stats[...]
    code_rest.wait_recv()
    codes_t[...] = (codes_mine[...].astype(F32) + codes_other[...].astype(F32)).T.astype(BF16)
    for copy in stat_sends:
        copy.wait_recv()
    got = [stats_in[i] for i in range(peers)]
    top_s, top_t = got[0][0:1], got[0][2:3]
    for one in got[1:]:
        top_s, top_t = jnp.maximum(top_s, one[0:1]), jnp.maximum(top_t, one[2:3])
    zs_sum = zt_sum = cross_sum = jnp.zeros_like(top_s)
    for one in got:
        zs_sum = zs_sum + one[1:2] * jnp.exp(one[0:1] - top_s)
        scale = jnp.exp(one[2:3] - top_t)
        zt_sum = zt_sum + one[3:4] * scale
        cross_sum = cross_sum + one[4:5] * scale
    log_zs = top_s + jnp.log(zs_sum)
    log_zt = top_t + jnp.log(zt_sum)
    kl_out[...] = cross_sum / zt_sum - log_zt + log_zs
    flip[...] = jnp.zeros_like(flip)
    flip[0:1, :] = log_zs
    flip[1:2, :] = log_zt
    flip[2:3, :] = counted[...].astype(F32) / rows
    cols = flip[...].T
    grad_half = (cols[:, 2:3] * (jnp.exp(student - cols[:, 0:1]) - jnp.exp(tl - cols[:, 1:2]))).astype(BF16)
    vh = vocab_size // 2
    my_blocks = pl.ds(p * vh, vh)
    grad[my_blocks] = grad_half.reshape(vh, token_size, block, columns)
    grad_pair = remote(grad.at[my_blocks], grad.at[my_blocks], pair_s.at[2], pair_r.at[2], mate)
    grad_pair.start()
    down_tok.wait_recv()
    arrived = d_all.at[pl.ds(pl.multiple_of((1 - t) * rank + v * share, share), share)]
    down_sends = []
    for k in range(1, vocab_size):
        down_sends.append(remote(arrived, arrived, dn_s.at[k], dn_r.at[k], {"vocab": lax.rem(v + k, vocab_size)}))
        down_sends[-1].start()
    grad_pair.wait_recv()

    group = vocab_size * block
    g_other = grad[:, 1 - t].reshape(group, columns)
    x_sends = []
    for j in range(PARTS):
        xs[j] = mm(g_other, w[pl.ds(j * part, part), :], NT).astype(BF16).reshape(vocab_size, block, part)
        x_sends.append(remote(xs.at[j], xr.at[j], xs_s.at[j], xs_r.at[j], across))
        x_sends[-1].start()
        if j == 0:
            g_all = grad[...].reshape(rows, columns)
            cgp[...] = (mm(g_all, up_v[...], NT) * mask[...]).astype(BF16).reshape(peers, block, rank2)
            cp_sends = []
            for k in range(1, peers):
                b, where = peer(k)
                cp_sends.append(remote(cgp.at[b], cgp_in.at[me], cp_s.at[k], cp_r.at[k], where))
                cp_sends[-1].start()
            cgp_in[me] = cgp[me]
    g_own = grad[:, t].reshape(group, columns)
    for j in range(PARTS):
        own[j] = mm(g_own, w[pl.ds(j * part, part), :], NT).reshape(vocab_size, block, part)

    up_out[...] = (ADAPTER_SCALE * mm(codes_t[...], g_all)).astype(BF16)

    z_sends = []
    for j in range(PARTS):
        if j == PARTS // 2:
            for copy in cp_sends:
                copy.wait_recv()
            total = cgp_in[0].astype(F32)
            for i in range(1, peers):
                total = total + cgp_in[i].astype(F32)
            cg_all[me] = total.astype(BF16)
            cg_sends = []
            for k in range(1, peers):
                cg_sends.append(remote(cg_all.at[me], cg_all.at[me], cg_s.at[k], cg_r.at[k], peer(k)[1]))
                cg_sends[-1].start()
        x_sends[j].wait_recv()
        merged = own[j] + xr[j].astype(F32)
        own[j] = merged
        zs[j] = merged.astype(BF16)
        for k in range(1, vocab_size):
            to = lax.rem(v + k, vocab_size)
            z_sends.append(remote(zs.at[j, to], zr.at[j, k], z_s.at[j, k], z_r.at[j, k], {"vocab": to}))
            z_sends[-1].start()
    for copy in cg_sends:
        copy.wait_recv()
    cg_t[...] = cg_all[...].reshape(rows, rank2).astype(F32).T.astype(BF16)
    down_out[...] = (ADAPTER_SCALE * mm(cg_t[at_rows(t, rank), :], h[...])).astype(BF16)

    for copy in down_sends:
        copy.wait_recv()
    my_cg = cg_all[me]
    for j in range(PARTS):
        for k in range(1, vocab_size):
            z_sends[j * (vocab_size - 1) + k - 1].wait_recv()
        value = own[j, v] + ADAPTER_SCALE * mm(my_cg, d_all[:, pl.ds(j * part, part)])
        for k in range(1, vocab_size):
            value = value + zr[j, k].astype(F32)
        hidden_out[:, pl.ds(j * part, part)] = value.astype(BF16)

    for copy in [code_pair, logit_pair, grad_pair, code_tok, code_rest, down_tok] + sends + forwards + down_sends + stat_sends + cp_sends + cg_sends + x_sends + z_sends:
        copy.wait_send()


def fused_shards(hidden, student_head_weight, down_weight, up_weight, teacher, tenant, counted_row_mask):
    vocab_size, token_size = lax.axis_size("vocab"), lax.axis_size("tokens")
    peers = vocab_size * token_size
    rows = tenant.shape[0]
    half = rows // 2
    block = rows // peers
    width, columns = student_head_weight.shape
    tenants, rank, _ = up_weight.shape
    rank2 = tenants * rank
    part = width // PARTS
    down_t = jnp.swapaxes(down_weight[0], 0, 1)
    vmem = pl.BlockSpec(memory_space=pltpu.VMEM)
    hbm = pl.BlockSpec(memory_space=pl.ANY)
    dma = pltpu.SemaphoreType.DMA
    kernel = functools.partial(fused, vocab_size, token_size)
    token_kl, hidden_gradient, down_gradient, up_gradient = pl.pallas_call(
        kernel,
        out_shape=(
            jax.ShapeDtypeStruct((1, half), F32),
            jax.ShapeDtypeStruct((block, width), BF16),
            jax.ShapeDtypeStruct((rank, width), BF16),
            jax.ShapeDtypeStruct((rank2, columns), BF16),
        ),
        in_specs=[hbm] * 5 + [vmem] * 2,
        out_specs=(vmem,) * 4,
        scratch_shapes=[
            pltpu.VMEM((rows, rank2), F32),
            pltpu.VMEM((rows, width), BF16),
            pltpu.VMEM((width, columns), BF16),
            pltpu.VMEM((rank2, width), BF16),
            pltpu.VMEM((rank2, width), BF16),
            pltpu.VMEM((rank2, columns), BF16),
            pltpu.VMEM((half, columns), BF16),
            pltpu.VMEM((rows, columns), F32),
            pltpu.VMEM((half, columns), F32),
            pltpu.VMEM((rows, rank2), F32),
            pltpu.VMEM((rows, rank2), F32),
            pltpu.VMEM((rows, rank2), BF16),
            pltpu.VMEM((rows, rank2), BF16),
            pltpu.VMEM((rank2, rows), BF16),
            pltpu.VMEM((8, half), F32),
            pltpu.VMEM((peers, 8, half), F32),
            pltpu.VMEM((128, half), F32),
            pltpu.VMEM((vocab_size, token_size, block, columns), BF16),
            pltpu.VMEM((peers, block, rank2), BF16),
            pltpu.VMEM((peers, block, rank2), BF16),
            pltpu.VMEM((peers, block, rank2), BF16),
            pltpu.VMEM((rank2, rows), BF16),
            pltpu.VMEM((PARTS, vocab_size, block, part), BF16),
            pltpu.VMEM((PARTS, vocab_size, block, part), BF16),
            pltpu.VMEM((PARTS, vocab_size, block, part), F32),
            pltpu.VMEM((PARTS, vocab_size, block, part), BF16),
            pltpu.VMEM((PARTS, vocab_size, block, part), BF16),
            dma((7,)), dma((PIECES,)), dma((PIECES,)), dma((PIECES,)), dma((PIECES,)), dma((3,)), dma((3,)), dma((3,)), dma((3,)),
            dma((peers,)), dma((peers,)), dma((peers,)), dma((peers,)), dma((peers,)), dma((peers,)),
            dma((vocab_size,)), dma((vocab_size,)), dma((PARTS,)), dma((PARTS,)), dma((PARTS, vocab_size)), dma((PARTS, vocab_size)),
        ],
        compiler_params=pltpu.CompilerParams(
            collective_id=0, has_side_effects=True, vmem_limit_bytes=60 << 20
        ),
    )(hidden, student_head_weight, down_t, up_weight.reshape(rank2, columns), teacher, tenant.reshape(1, rows),
      counted_row_mask.reshape(1, half))
    return (
        token_kl.reshape(half),
        hidden_gradient,
        jnp.swapaxes(down_gradient, 0, 1)[None],
        up_gradient.reshape(tenants, rank, columns),
    )


def fits(mesh):
    return mesh.shape["tokens"] == 2 and mesh.shape["vocab"] == 4


def solution(mesh):
    return jax.shard_map(
        fused_shards if fits(mesh) else shards,
        mesh=mesh,
        in_specs=(
            P(("groups", "tokens"), "pair"),
            P("pair", ("vocab", "tokens")),
            P("tokens", "pair", None),
            P(None, None, ("vocab", "tokens")),
            P(("groups", "pair"), ("vocab", "tokens")),
            P("groups"),
            P(("groups", "pair")),
        ),
        out_specs=(
            P(("groups", "pair")),
            P(("groups", "vocab", "tokens"), "pair"),
            P(("groups", "tokens"), "pair", None),
            P("groups", None, ("vocab", "tokens")),
        ),
        check_vma=False,
    )
```

```python
import functools

import jax
import jax.numpy as jnp
from jax import lax
from jax.experimental import pallas as pl
from jax.experimental.pallas import tpu as pltpu
from jax.sharding import PartitionSpec as P

BLOCK = 64


ADAPTER_SCALE = 0.5


def shards(hidden, student_head_weight, down_weight, up_weight, teacher, tenant, counted_row_mask):
    all_rows = tenant.shape[0]
    half_rows = all_rows // lax.axis_size("pair")
    pair_index = lax.axis_index("pair")
    block_count = all_rows // BLOCK
    half_blocks = half_rows // BLOCK
    tenant_per_block = tenant.reshape(block_count, BLOCK)[:, 0]
    gathered = lax.all_gather(hidden, "tokens", axis=0, tiled=True)
    width = gathered.shape[1]
    adapter_rank = down_weight.shape[2]
    columns = student_head_weight.shape[1]
    tenant_number = up_weight.shape[0]
    owner_mask = tenant == lax.axis_index("tokens")
    lookup_tables = lax.all_gather(down_weight, "tokens", axis=0, tiled=True)
    selected_down = lookup_tables[tenant_per_block]
    partial_codes = jnp.einsum(
        "nmw,nwz->nmz",
        gathered.reshape(block_count, BLOCK, width),
        selected_down,
        preferred_element_type=jnp.float32,
    ).reshape(all_rows, adapter_rank)
    summed_codes = lax.psum(partial_codes, "pair")
    adapter_codes = summed_codes.astype(jnp.bfloat16)
    slab = gathered
    trunk_logits = lax.psum_scatter(
        jnp.dot(slab, student_head_weight, preferred_element_type=jnp.float32),
        "pair",
        scatter_dimension=0,
        tiled=True,
    )
    my_codes = lax.dynamic_slice_in_dim(adapter_codes, pair_index * half_rows, half_rows, 0)
    local_tenant = lax.dynamic_slice_in_dim(
        tenant_per_block, pair_index * half_blocks, half_blocks, 0
    )
    adapter_logits = jnp.einsum(
        "gji,giu->gju",
        my_codes.reshape(half_blocks, BLOCK, adapter_rank),
        up_weight[local_tenant],
        preferred_element_type=jnp.float32,
    ).reshape(half_rows, columns)
    student_model = trunk_logits + ADAPTER_SCALE * adapter_logits
    teacher_logits = teacher.astype(jnp.float32)
    peak_s, peak_t = lax.pmax(
        (jnp.max(student_model, axis=1), jnp.max(teacher_logits, axis=1)), ("vocab", "tokens")
    )
    exp_t = jnp.exp(teacher_logits - peak_t[:, None])
    sum_s, sum_t, cross_sum = lax.psum(
        (
            jnp.sum(jnp.exp(student_model - peak_s[:, None]), axis=1),
            jnp.sum(exp_t, axis=1),
            jnp.sum(exp_t * (teacher_logits - student_model), axis=1),
        ),
        ("vocab", "tokens"),
    )
    log_zs = peak_s + jnp.log(sum_s)
    log_zt = peak_t + jnp.log(sum_t)
    token_kl = cross_sum / sum_t - log_zt + log_zs
    weights = counted_row_mask.astype(jnp.float32) / all_rows
    grad_half = (
        weights[:, None]
        * (jnp.exp(student_model - log_zs[:, None]) - jnp.exp(teacher_logits - log_zt[:, None]))
    ).astype(jnp.bfloat16)
    full_grad = lax.all_gather(grad_half, "pair", axis=0, tiled=True)
    grad_blocks = full_grad.reshape(block_count, BLOCK, columns)
    selected_up = up_weight[tenant_per_block]
    code_part = jnp.einsum(
        "bkv,brv->bkr", grad_blocks, selected_up, preferred_element_type=jnp.float32
    ).reshape(all_rows, adapter_rank)
    code_gradient = lax.psum(code_part, ("vocab", "tokens")).astype(jnp.bfloat16)
    up_outer_product = jnp.einsum(
        "bkr,bkv->brv",
        adapter_codes.reshape(block_count, BLOCK, adapter_rank),
        grad_blocks,
        preferred_element_type=jnp.float32,
    )
    tenant_onehot = (tenant_per_block[:, None] == jnp.arange(tenant_number)[None, :]).astype(
        jnp.float32
    )
    up_gradient = (
        ADAPTER_SCALE
        * jnp.einsum(
            "yf,ysk->fsk", tenant_onehot, up_outer_product, precision=lax.Precision.HIGHEST
        )
    ).astype(jnp.bfloat16)
    owned_grad = jnp.where(owner_mask[:, None], code_gradient, jnp.zeros_like(code_gradient))
    down_gradient = (
        ADAPTER_SCALE
        * jnp.einsum("kd,kr->dr", gathered, owned_grad, preferred_element_type=jnp.float32)
    )[None].astype(jnp.bfloat16)
    shard_rows = all_rows // lax.axis_size(("vocab", "tokens"))
    slab = full_grad
    total = jnp.einsum("kv,dv->kd", slab, student_head_weight, preferred_element_type=jnp.float32)
    width_gradients = lax.psum_scatter(total, ("vocab", "tokens"), scatter_dimension=0, tiled=True)
    row_start = lax.axis_index(("vocab", "tokens")) * shard_rows
    my_grad_codes = lax.dynamic_slice_in_dim(code_gradient, row_start, shard_rows, 0)
    my_row_tenant = lax.dynamic_slice_in_dim(tenant, row_start, shard_rows, 0)
    width_gradients = width_gradients + ADAPTER_SCALE * jnp.einsum(
        "kr,kdr->kd",
        my_grad_codes,
        lookup_tables[my_row_tenant],
        preferred_element_type=jnp.float32,
    )
    hidden_gradient = width_gradients.astype(jnp.bfloat16)
    return (token_kl, hidden_gradient, down_gradient, up_gradient)


F32 = jnp.float32
BF16 = jnp.bfloat16
PARTS = 10
PIECES = 4
NT = (((1,), (1,)), ((), ()))
NN = (((1,), (0,)), ((), ()))


def mm(a, b, dims=NN):
    return lax.dot_general(a, b, dims, preferred_element_type=F32)


def remote(src, dst, send, recv, where):
    return pltpu.make_async_remote_copy(
        src_ref=src, dst_ref=dst, send_sem=send, recv_sem=recv,
        device_id=where, device_id_type=pl.DeviceIdType.MESH,
    )


def fused(
    vocab_size, token_size,
    hidden, weight, down_t, up, teacher, tenant, counted,
    kl_out, hidden_out, down_out, up_out,
    mask, h, w, d_dup, d_all, up_v, teach, acc, acc_in,
    code_part, code_in, codes_mine, codes_other, codes_t,
    stats, stats_in, flip, grad, cgp, cgp_in, cg_all, cg_t,
    xs, xr, own, zs, zr,
    lsem, hs, hr, fs, fr, pair_s, pair_r, tok_s, tok_r,
    st_s, st_r, cp_s, cp_r, cg_s, cg_r, dn_s, dn_r, xs_s, xs_r, z_s, z_r,
):
    v, t, p = lax.axis_index("vocab"), lax.axis_index("tokens"), lax.axis_index("pair")
    peers = vocab_size * token_size
    me = v * token_size + t
    mate = {"pair": 1 - p}
    across = {"tokens": 1 - t}
    rows, rank2 = mask.shape
    half = rows // 2
    rank = rank2 // 2
    columns = weight.shape[1]
    width = weight.shape[0]
    part = width // PARTS
    block = rows // peers

    def peer(k):
        b = lax.rem(me + k, peers)
        return b, {"vocab": b // token_size, "tokens": lax.rem(b, token_size)}

    def at_rows(i, n):
        return pl.ds(pl.multiple_of(i * n, n), n)

    local = [
        pltpu.make_async_copy(hidden, h.at[at_rows(t, half)], lsem.at[0]),
        pltpu.make_async_copy(weight, w, lsem.at[1]),
        pltpu.make_async_copy(down_t, d_dup.at[pl.ds(0, rank)], lsem.at[2]),
        pltpu.make_async_copy(down_t, d_dup.at[pl.ds(rank, rank)], lsem.at[3]),
        pltpu.make_async_copy(down_t, d_all.at[at_rows(t, rank)], lsem.at[4]),
        pltpu.make_async_copy(up, up_v, lsem.at[5]),
        pltpu.make_async_copy(teacher, teach, lsem.at[6]),
    ]
    for copy in local:
        copy.start()

    barrier = pltpu.get_barrier_semaphore()
    pl.semaphore_signal(barrier, inc=1, device_id=mate, device_id_type=pl.DeviceIdType.MESH)
    for k in range(1, peers):
        pl.semaphore_signal(barrier, inc=1, device_id=peer(k)[1], device_id_type=pl.DeviceIdType.MESH)
    pl.semaphore_wait(barrier, peers)

    quarter = half // 2
    piece_rows = quarter // PIECES
    odd = lax.rem(v, 2)
    neighbour = {"vocab": v + 1 - 2 * odd}
    sends, forwards = [], []
    for c in range(PIECES):
        start = odd * quarter + c * piece_rows
        sends.append(remote(
            hidden.at[pl.ds(pl.multiple_of(start, piece_rows), piece_rows)],
            h.at[pl.ds(pl.multiple_of(t * half + start, piece_rows), piece_rows)],
            hs.at[c], hr.at[c], across,
        ))
        sends[-1].start()

    tenant_of = lax.broadcasted_iota(jnp.int32, (rank2, rows), 0) // rank
    mask[...] = (tenant_of == tenant[...]).astype(F32).T

    for copy in local:
        copy.wait()

    own_lane = (lax.broadcasted_iota(jnp.int32, (1, rank2), 1) // rank == t).astype(F32)

    def forward(start, n):
        sl = pl.ds(pl.multiple_of(start, n), n)
        piece = h[sl, :]
        code_part[sl, :] = mm(piece, d_dup[...], NT) * mask[sl, :] * own_lane
        return sl, piece

    sl, piece = forward(t * half, half)
    acc[sl, :] = mm(piece, w[...])
    mate_rows = at_rows(1 - p, half)
    my_rows = at_rows(p, half)

    def logit_piece(q, i):
        there = pl.ds(pl.multiple_of((1 - p) * half + q * quarter, quarter), quarter)
        return remote(acc.at[there], acc_in.at[at_rows(q, quarter)], pair_s.at[i], pair_r.at[i], mate)

    for c in range(PIECES):
        sends[c].wait_recv()
        start = pl.multiple_of((1 - t) * half + odd * quarter + c * piece_rows, piece_rows)
        there = h.at[pl.ds(start, piece_rows)]
        forwards.append(remote(there, there, fs.at[c], fr.at[c], neighbour))
        forwards[-1].start()
    sl, piece = forward((1 - t) * half + odd * quarter, quarter)
    acc[sl, :] = mm(piece, w[...])
    logit_pair = logit_piece(odd, 1)
    logit_pair.start()
    for copy in forwards:
        copy.wait_recv()
    sl, piece = forward((1 - t) * half + (1 - odd) * quarter, quarter)
    code_pair = remote(code_part, code_in, pair_s.at[0], pair_r.at[0], mate)
    code_pair.start()
    acc[sl, :] = mm(piece, w[...])
    logit_last = logit_piece(1 - odd, 3)
    logit_last.start()
    code_pair.wait_recv()
    codes_mine[...] = (code_part[...] + code_in[...]).astype(BF16)
    code_tok = remote(codes_mine.at[my_rows], codes_other.at[my_rows], tok_s.at[0], tok_r.at[0], across)
    code_tok.start()
    code_rest = remote(codes_mine.at[mate_rows], codes_other.at[mate_rows], tok_s.at[2], tok_r.at[2], across)
    code_rest.start()
    share = rank // vocab_size
    sent = pl.ds(pl.multiple_of(t * rank + v * share, share), share)
    down_tok = remote(d_dup.at[at_rows(v, share)], d_all.at[sent], tok_s.at[1], tok_r.at[1], across)
    down_tok.start()

    tl = teach[...].astype(F32)
    peak_t = jnp.max(tl, axis=1, keepdims=True)
    exp_t = jnp.exp(tl - peak_t)
    sum_t = jnp.sum(exp_t, axis=1, keepdims=True)

    logit_pair.wait_recv()
    logit_last.wait_recv()
    code_tok.wait_recv()
    codes_mine_half = (codes_mine[my_rows, :].astype(F32) + codes_other[my_rows, :].astype(F32)).astype(BF16)
    student = acc[my_rows, :] + acc_in[...] + ADAPTER_SCALE * mm(codes_mine_half, up_v[...])
    peak_s = jnp.max(student, axis=1, keepdims=True)
    sum_s = jnp.sum(jnp.exp(student - peak_s), axis=1, keepdims=True)
    cross = jnp.sum(exp_t * (tl - student), axis=1, keepdims=True)

    lane = lax.broadcasted_iota(jnp.int32, (half, 128), 1)
    packed = jnp.zeros((half, 128), F32)
    for i, value in enumerate((peak_s, sum_s, peak_t, sum_t, cross)):
        packed = jnp.where(lane == i, value, packed)
    stats[...] = packed.T[:8, :]
    stat_sends = []
    for k in range(1, peers):
        stat_sends.append(remote(stats, stats_in.at[me], st_s.at[k], st_r.at[k], peer(k)[1]))
        stat_sends[-1].start()
    stats_in[me] = stats[...]
    code_rest.wait_recv()
    codes_t[...] = (codes_mine[...].astype(F32) + codes_other[...].astype(F32)).T.astype(BF16)
    for copy in stat_sends:
        copy.wait_recv()
    got = [stats_in[i] for i in range(peers)]
    top_s, top_t = got[0][0:1], got[0][2:3]
    for one in got[1:]:
        top_s, top_t = jnp.maximum(top_s, one[0:1]), jnp.maximum(top_t, one[2:3])
    zs_sum = zt_sum = cross_sum = jnp.zeros_like(top_s)
    for one in got:
        zs_sum = zs_sum + one[1:2] * jnp.exp(one[0:1] - top_s)
        scale = jnp.exp(one[2:3] - top_t)
        zt_sum = zt_sum + one[3:4] * scale
        cross_sum = cross_sum + one[4:5] * scale
    log_zs = top_s + jnp.log(zs_sum)
    log_zt = top_t + jnp.log(zt_sum)
    kl_out[...] = cross_sum / zt_sum - log_zt + log_zs
    flip[...] = jnp.zeros_like(flip)
    flip[0:1, :] = log_zs
    flip[1:2, :] = log_zt
    flip[2:3, :] = counted[...].astype(F32) / rows
    cols = flip[...].T
    grad_half = (cols[:, 2:3] * (jnp.exp(student - cols[:, 0:1]) - jnp.exp(tl - cols[:, 1:2]))).astype(BF16)
    vh = vocab_size // 2
    my_blocks = pl.ds(p * vh, vh)
    grad[my_blocks] = grad_half.reshape(vh, token_size, block, columns)
    grad_pair = remote(grad.at[my_blocks], grad.at[my_blocks], pair_s.at[2], pair_r.at[2], mate)
    grad_pair.start()
    down_tok.wait_recv()
    arrived = d_all.at[pl.ds(pl.multiple_of((1 - t) * rank + v * share, share), share)]
    down_sends = []
    for k in range(1, vocab_size):
        down_sends.append(remote(arrived, arrived, dn_s.at[k], dn_r.at[k], {"vocab": lax.rem(v + k, vocab_size)}))
        down_sends[-1].start()
    grad_pair.wait_recv()

    group = vocab_size * block
    g_other = grad[:, 1 - t].reshape(group, columns)
    x_sends = []
    for j in range(PARTS):
        xs[j] = mm(g_other, w[pl.ds(j * part, part), :], NT).astype(BF16).reshape(vocab_size, block, part)
        x_sends.append(remote(xs.at[j], xr.at[j], xs_s.at[j], xs_r.at[j], across))
        x_sends[-1].start()
        if j == 0:
            g_all = grad[...].reshape(rows, columns)
            cgp[...] = (mm(g_all, up_v[...], NT) * mask[...]).astype(BF16).reshape(peers, block, rank2)
            cp_sends = []
            for k in range(1, peers):
                b, where = peer(k)
                cp_sends.append(remote(cgp.at[b], cgp_in.at[me], cp_s.at[k], cp_r.at[k], where))
                cp_sends[-1].start()
            cgp_in[me] = cgp[me]
    g_own = grad[:, t].reshape(group, columns)
    for j in range(PARTS):
        own[j] = mm(g_own, w[pl.ds(j * part, part), :], NT).reshape(vocab_size, block, part)

    up_out[...] = (ADAPTER_SCALE * mm(codes_t[...], g_all)).astype(BF16)

    z_sends = []
    for j in range(PARTS):
        if j == PARTS // 2:
            for copy in cp_sends:
                copy.wait_recv()
            total = cgp_in[0].astype(F32)
            for i in range(1, peers):
                total = total + cgp_in[i].astype(F32)
            cg_all[me] = total.astype(BF16)
            cg_sends = []
            for k in range(1, peers):
                cg_sends.append(remote(cg_all.at[me], cg_all.at[me], cg_s.at[k], cg_r.at[k], peer(k)[1]))
                cg_sends[-1].start()
        x_sends[j].wait_recv()
        merged = own[j] + xr[j].astype(F32)
        own[j] = merged
        zs[j] = merged.astype(BF16)
        for k in range(1, vocab_size):
            to = lax.rem(v + k, vocab_size)
            z_sends.append(remote(zs.at[j, to], zr.at[j, k], z_s.at[j, k], z_r.at[j, k], {"vocab": to}))
            z_sends[-1].start()
    for copy in cg_sends:
        copy.wait_recv()
    cg_t[...] = cg_all[...].reshape(rows, rank2).astype(F32).T.astype(BF16)
    down_out[...] = (ADAPTER_SCALE * mm(cg_t[at_rows(t, rank), :], h[...])).astype(BF16)

    for copy in down_sends:
        copy.wait_recv()
    my_cg = cg_all[me]
    for j in range(PARTS):
        for k in range(1, vocab_size):
            z_sends[j * (vocab_size - 1) + k - 1].wait_recv()
        value = own[j, v] + ADAPTER_SCALE * mm(my_cg, d_all[:, pl.ds(j * part, part)])
        for k in range(1, vocab_size):
            value = value + zr[j, k].astype(F32)
        hidden_out[:, pl.ds(j * part, part)] = value.astype(BF16)

    for copy in [code_pair, logit_pair, logit_last, grad_pair, code_tok, code_rest, down_tok] + sends + forwards + down_sends + stat_sends + cp_sends + cg_sends + x_sends + z_sends:
        copy.wait_send()


def hand_over(a, b, c, d, a_out, b_out, c_out, d_out, sem):
    copies = [
        pltpu.make_async_copy(source, target, sem.at[i])
        for i, (source, target) in enumerate(((a, a_out), (b, b_out), (c, c_out), (d, d_out)))
    ]
    for copy in copies:
        copy.start()
    for copy in copies:
        copy.wait()


def fused_shards(hidden, student_head_weight, down_weight, up_weight, teacher, tenant, counted_row_mask):
    vocab_size, token_size = lax.axis_size("vocab"), lax.axis_size("tokens")
    peers = vocab_size * token_size
    rows = tenant.shape[0]
    half = rows // 2
    block = rows // peers
    width, columns = student_head_weight.shape
    tenants, rank, _ = up_weight.shape
    rank2 = tenants * rank
    part = width // PARTS
    down_t = jnp.swapaxes(down_weight[0], 0, 1)
    vmem = pl.BlockSpec(memory_space=pltpu.VMEM)
    hbm = pl.BlockSpec(memory_space=pl.ANY)
    dma = pltpu.SemaphoreType.DMA
    kernel = functools.partial(fused, vocab_size, token_size)
    token_kl, hidden_gradient, down_gradient, up_gradient = pl.pallas_call(
        kernel,
        out_shape=(
            jax.ShapeDtypeStruct((1, half), F32),
            jax.ShapeDtypeStruct((block, width), BF16),
            jax.ShapeDtypeStruct((rank, width), BF16),
            jax.ShapeDtypeStruct((rank2, columns), BF16),
        ),
        in_specs=[hbm] * 5 + [vmem] * 2,
        out_specs=(vmem,) * 4,
        scratch_shapes=[
            pltpu.VMEM((rows, rank2), F32),
            pltpu.VMEM((rows, width), BF16),
            pltpu.VMEM((width, columns), BF16),
            pltpu.VMEM((rank2, width), BF16),
            pltpu.VMEM((rank2, width), BF16),
            pltpu.VMEM((rank2, columns), BF16),
            pltpu.VMEM((half, columns), BF16),
            pltpu.VMEM((rows, columns), F32),
            pltpu.VMEM((half, columns), F32),
            pltpu.VMEM((rows, rank2), F32),
            pltpu.VMEM((rows, rank2), F32),
            pltpu.VMEM((rows, rank2), BF16),
            pltpu.VMEM((rows, rank2), BF16),
            pltpu.VMEM((rank2, rows), BF16),
            pltpu.VMEM((8, half), F32),
            pltpu.VMEM((peers, 8, half), F32),
            pltpu.VMEM((128, half), F32),
            pltpu.VMEM((vocab_size, token_size, block, columns), BF16),
            pltpu.VMEM((peers, block, rank2), BF16),
            pltpu.VMEM((peers, block, rank2), BF16),
            pltpu.VMEM((peers, block, rank2), BF16),
            pltpu.VMEM((rank2, rows), BF16),
            pltpu.VMEM((PARTS, vocab_size, block, part), BF16),
            pltpu.VMEM((PARTS, vocab_size, block, part), BF16),
            pltpu.VMEM((PARTS, vocab_size, block, part), F32),
            pltpu.VMEM((PARTS, vocab_size, block, part), BF16),
            pltpu.VMEM((PARTS, vocab_size, block, part), BF16),
            dma((7,)), dma((PIECES,)), dma((PIECES,)), dma((PIECES,)), dma((PIECES,)), dma((4,)), dma((4,)), dma((3,)), dma((3,)),
            dma((peers,)), dma((peers,)), dma((peers,)), dma((peers,)), dma((peers,)), dma((peers,)),
            dma((vocab_size,)), dma((vocab_size,)), dma((PARTS,)), dma((PARTS,)), dma((PARTS, vocab_size)), dma((PARTS, vocab_size)),
        ],
        compiler_params=pltpu.CompilerParams(
            collective_id=0, has_side_effects=True, vmem_limit_bytes=60 << 20
        ),
    )(hidden, student_head_weight, down_t, up_weight.reshape(rank2, columns), teacher, tenant.reshape(1, rows),
      counted_row_mask.reshape(1, half))
    made = (token_kl, hidden_gradient, down_gradient, up_gradient)
    token_kl, hidden_gradient, down_gradient, up_gradient = pl.pallas_call(
        hand_over,
        out_shape=tuple(jax.ShapeDtypeStruct(one.shape, one.dtype) for one in made),
        in_specs=[hbm] * 4,
        out_specs=(hbm,) * 4,
        scratch_shapes=[dma((4,))],
        compiler_params=pltpu.CompilerParams(vmem_limit_bytes=60 << 20),
    )(*made)
    return (
        token_kl.reshape(half),
        hidden_gradient,
        jnp.swapaxes(down_gradient, 0, 1)[None],
        up_gradient.reshape(tenants, rank, columns),
    )


def fits(mesh):
    return mesh.shape["tokens"] == 2 and mesh.shape["vocab"] == 4


def solution(mesh):
    return jax.shard_map(
        fused_shards if fits(mesh) else shards,
        mesh=mesh,
        in_specs=(
            P(("groups", "tokens"), "pair"),
            P("pair", ("vocab", "tokens")),
            P("tokens", "pair", None),
            P(None, None, ("vocab", "tokens")),
            P(("groups", "pair"), ("vocab", "tokens")),
            P("groups"),
            P(("groups", "pair")),
        ),
        out_specs=(
            P(("groups", "pair")),
            P(("groups", "vocab", "tokens"), "pair"),
            P(("groups", "tokens"), "pair", None),
            P("groups", None, ("vocab", "tokens")),
        ),
        check_vma=False,
    )
```

```python
import functools

import jax
import jax.numpy as jnp
from jax import lax
from jax.experimental import pallas as pl
from jax.experimental.pallas import tpu as pltpu
from jax.sharding import PartitionSpec as P

BLOCK = 64


ADAPTER_SCALE = 0.5


def shards(hidden, student_head_weight, down_weight, up_weight, teacher, tenant, counted_row_mask):
    all_rows = tenant.shape[0]
    half_rows = all_rows // lax.axis_size("pair")
    pair_index = lax.axis_index("pair")
    block_count = all_rows // BLOCK
    half_blocks = half_rows // BLOCK
    tenant_per_block = tenant.reshape(block_count, BLOCK)[:, 0]
    gathered = lax.all_gather(hidden, "tokens", axis=0, tiled=True)
    width = gathered.shape[1]
    adapter_rank = down_weight.shape[2]
    columns = student_head_weight.shape[1]
    tenant_number = up_weight.shape[0]
    owner_mask = tenant == lax.axis_index("tokens")
    lookup_tables = lax.all_gather(down_weight, "tokens", axis=0, tiled=True)
    selected_down = lookup_tables[tenant_per_block]
    partial_codes = jnp.einsum(
        "nmw,nwz->nmz",
        gathered.reshape(block_count, BLOCK, width),
        selected_down,
        preferred_element_type=jnp.float32,
    ).reshape(all_rows, adapter_rank)
    summed_codes = lax.psum(partial_codes, "pair")
    adapter_codes = summed_codes.astype(jnp.bfloat16)
    slab = gathered
    trunk_logits = lax.psum_scatter(
        jnp.dot(slab, student_head_weight, preferred_element_type=jnp.float32),
        "pair",
        scatter_dimension=0,
        tiled=True,
    )
    my_codes = lax.dynamic_slice_in_dim(adapter_codes, pair_index * half_rows, half_rows, 0)
    local_tenant = lax.dynamic_slice_in_dim(
        tenant_per_block, pair_index * half_blocks, half_blocks, 0
    )
    adapter_logits = jnp.einsum(
        "gji,giu->gju",
        my_codes.reshape(half_blocks, BLOCK, adapter_rank),
        up_weight[local_tenant],
        preferred_element_type=jnp.float32,
    ).reshape(half_rows, columns)
    student_model = trunk_logits + ADAPTER_SCALE * adapter_logits
    teacher_logits = teacher.astype(jnp.float32)
    peak_s, peak_t = lax.pmax(
        (jnp.max(student_model, axis=1), jnp.max(teacher_logits, axis=1)), ("vocab", "tokens")
    )
    exp_t = jnp.exp(teacher_logits - peak_t[:, None])
    sum_s, sum_t, cross_sum = lax.psum(
        (
            jnp.sum(jnp.exp(student_model - peak_s[:, None]), axis=1),
            jnp.sum(exp_t, axis=1),
            jnp.sum(exp_t * (teacher_logits - student_model), axis=1),
        ),
        ("vocab", "tokens"),
    )
    log_zs = peak_s + jnp.log(sum_s)
    log_zt = peak_t + jnp.log(sum_t)
    token_kl = cross_sum / sum_t - log_zt + log_zs
    weights = counted_row_mask.astype(jnp.float32) / all_rows
    grad_half = (
        weights[:, None]
        * (jnp.exp(student_model - log_zs[:, None]) - jnp.exp(teacher_logits - log_zt[:, None]))
    ).astype(jnp.bfloat16)
    full_grad = lax.all_gather(grad_half, "pair", axis=0, tiled=True)
    grad_blocks = full_grad.reshape(block_count, BLOCK, columns)
    selected_up = up_weight[tenant_per_block]
    code_part = jnp.einsum(
        "bkv,brv->bkr", grad_blocks, selected_up, preferred_element_type=jnp.float32
    ).reshape(all_rows, adapter_rank)
    code_gradient = lax.psum(code_part, ("vocab", "tokens")).astype(jnp.bfloat16)
    up_outer_product = jnp.einsum(
        "bkr,bkv->brv",
        adapter_codes.reshape(block_count, BLOCK, adapter_rank),
        grad_blocks,
        preferred_element_type=jnp.float32,
    )
    tenant_onehot = (tenant_per_block[:, None] == jnp.arange(tenant_number)[None, :]).astype(
        jnp.float32
    )
    up_gradient = (
        ADAPTER_SCALE
        * jnp.einsum(
            "yf,ysk->fsk", tenant_onehot, up_outer_product, precision=lax.Precision.HIGHEST
        )
    ).astype(jnp.bfloat16)
    owned_grad = jnp.where(owner_mask[:, None], code_gradient, jnp.zeros_like(code_gradient))
    down_gradient = (
        ADAPTER_SCALE
        * jnp.einsum("kd,kr->dr", gathered, owned_grad, preferred_element_type=jnp.float32)
    )[None].astype(jnp.bfloat16)
    shard_rows = all_rows // lax.axis_size(("vocab", "tokens"))
    slab = full_grad
    total = jnp.einsum("kv,dv->kd", slab, student_head_weight, preferred_element_type=jnp.float32)
    width_gradients = lax.psum_scatter(total, ("vocab", "tokens"), scatter_dimension=0, tiled=True)
    row_start = lax.axis_index(("vocab", "tokens")) * shard_rows
    my_grad_codes = lax.dynamic_slice_in_dim(code_gradient, row_start, shard_rows, 0)
    my_row_tenant = lax.dynamic_slice_in_dim(tenant, row_start, shard_rows, 0)
    width_gradients = width_gradients + ADAPTER_SCALE * jnp.einsum(
        "kr,kdr->kd",
        my_grad_codes,
        lookup_tables[my_row_tenant],
        preferred_element_type=jnp.float32,
    )
    hidden_gradient = width_gradients.astype(jnp.bfloat16)
    return (token_kl, hidden_gradient, down_gradient, up_gradient)


F32 = jnp.float32
BF16 = jnp.bfloat16
PARTS = 10
PIECES = 4
NT = (((1,), (1,)), ((), ()))
NN = (((1,), (0,)), ((), ()))


def mm(a, b, dims=NN):
    return lax.dot_general(a, b, dims, preferred_element_type=F32)


def remote(src, dst, send, recv, where):
    return pltpu.make_async_remote_copy(
        src_ref=src, dst_ref=dst, send_sem=send, recv_sem=recv,
        device_id=where, device_id_type=pl.DeviceIdType.MESH,
    )


def fused(
    vocab_size, token_size,
    hidden, weight, down_t, up, teacher, tenant, counted,
    kl_out, hidden_out, down_out, up_out,
    mask, h, w, d_dup, d_all, up_v, teach, acc, acc_in,
    code_part, code_in, codes_mine, codes_other, codes_t,
    stats, stats_in, flip, grad, cgp, cgp_in, cg_all, cg_t,
    xs, xr, own, zs, zr,
    lsem, hs, hr, fs, fr, pair_s, pair_r, tok_s, tok_r,
    st_s, st_r, cp_s, cp_r, cg_s, cg_r, dn_s, dn_r, xs_s, xs_r, z_s, z_r,
):
    v, t, p = lax.axis_index("vocab"), lax.axis_index("tokens"), lax.axis_index("pair")
    peers = vocab_size * token_size
    me = v * token_size + t
    mate = {"pair": 1 - p}
    across = {"tokens": 1 - t}
    rows, rank2 = mask.shape
    half = rows // 2
    rank = rank2 // 2
    columns = weight.shape[1]
    width = weight.shape[0]
    part = width // PARTS
    block = rows // peers

    def peer(k):
        b = lax.rem(me + k, peers)
        return b, {"vocab": b // token_size, "tokens": lax.rem(b, token_size)}

    def at_rows(i, n):
        return pl.ds(pl.multiple_of(i * n, n), n)

    local = [
        pltpu.make_async_copy(hidden, h.at[at_rows(t, half)], lsem.at[0]),
        pltpu.make_async_copy(weight, w, lsem.at[1]),
        pltpu.make_async_copy(down_t, d_dup.at[pl.ds(0, rank)], lsem.at[2]),
        pltpu.make_async_copy(down_t, d_dup.at[pl.ds(rank, rank)], lsem.at[3]),
        pltpu.make_async_copy(down_t, d_all.at[at_rows(t, rank)], lsem.at[4]),
        pltpu.make_async_copy(up, up_v, lsem.at[5]),
        pltpu.make_async_copy(teacher, teach, lsem.at[6]),
    ]
    for copy in local:
        copy.start()

    barrier = pltpu.get_barrier_semaphore()
    pl.semaphore_signal(barrier, inc=1, device_id=mate, device_id_type=pl.DeviceIdType.MESH)
    for k in range(1, peers):
        pl.semaphore_signal(barrier, inc=1, device_id=peer(k)[1], device_id_type=pl.DeviceIdType.MESH)
    pl.semaphore_wait(barrier, peers)

    quarter = half // 2
    piece_rows = quarter // PIECES
    odd = lax.rem(v, 2)
    neighbour = {"vocab": v + 1 - 2 * odd}
    sends, forwards = [], []
    for c in range(PIECES):
        start = odd * quarter + c * piece_rows
        sends.append(remote(
            hidden.at[pl.ds(pl.multiple_of(start, piece_rows), piece_rows)],
            h.at[pl.ds(pl.multiple_of(t * half + start, piece_rows), piece_rows)],
            hs.at[c], hr.at[c], across,
        ))
        sends[-1].start()

    tenant_of = lax.broadcasted_iota(jnp.int32, (rank2, rows), 0) // rank
    mask[...] = (tenant_of == tenant[...]).astype(F32).T

    for copy in local:
        copy.wait()

    own_lane = (lax.broadcasted_iota(jnp.int32, (1, rank2), 1) // rank == t).astype(F32)

    def forward(start, n):
        sl = pl.ds(pl.multiple_of(start, n), n)
        piece = h[sl, :]
        code_part[sl, :] = mm(piece, d_dup[...], NT) * mask[sl, :] * own_lane
        return sl, piece

    sl, piece = forward(t * half, half)
    acc[sl, :] = mm(piece, w[...])
    mate_rows = at_rows(1 - p, half)
    my_rows = at_rows(p, half)

    def logit_piece(q, i):
        there = pl.ds(pl.multiple_of((1 - p) * half + q * quarter, quarter), quarter)
        return remote(acc.at[there], acc_in.at[at_rows(q, quarter)], pair_s.at[i], pair_r.at[i], mate)

    for c in range(PIECES):
        sends[c].wait_recv()
        start = pl.multiple_of((1 - t) * half + odd * quarter + c * piece_rows, piece_rows)
        there = h.at[pl.ds(start, piece_rows)]
        forwards.append(remote(there, there, fs.at[c], fr.at[c], neighbour))
        forwards[-1].start()
    sl, piece = forward((1 - t) * half + odd * quarter, quarter)
    acc[sl, :] = mm(piece, w[...])
    logit_pair = logit_piece(odd, 1)
    logit_pair.start()
    for copy in forwards:
        copy.wait_recv()
    sl, piece = forward((1 - t) * half + (1 - odd) * quarter, quarter)
    code_pair = remote(code_part, code_in, pair_s.at[0], pair_r.at[0], mate)
    code_pair.start()
    acc[sl, :] = mm(piece, w[...])
    logit_last = logit_piece(1 - odd, 3)
    logit_last.start()
    code_pair.wait_recv()
    codes_mine[...] = (code_part[...] + code_in[...]).astype(BF16)
    code_tok = remote(codes_mine.at[my_rows], codes_other.at[my_rows], tok_s.at[0], tok_r.at[0], across)
    code_tok.start()
    code_rest = remote(codes_mine.at[mate_rows], codes_other.at[mate_rows], tok_s.at[2], tok_r.at[2], across)
    code_rest.start()
    share = rank // vocab_size
    sent = pl.ds(pl.multiple_of(t * rank + v * share, share), share)
    down_tok = remote(d_dup.at[at_rows(v, share)], d_all.at[sent], tok_s.at[1], tok_r.at[1], across)
    down_tok.start()

    tl = teach[...].astype(F32)
    peak_t = jnp.max(tl, axis=1, keepdims=True)
    exp_t = jnp.exp(tl - peak_t)
    sum_t = jnp.sum(exp_t, axis=1, keepdims=True)

    logit_pair.wait_recv()
    logit_last.wait_recv()
    code_tok.wait_recv()
    codes_mine_half = (codes_mine[my_rows, :].astype(F32) + codes_other[my_rows, :].astype(F32)).astype(BF16)
    student = acc[my_rows, :] + acc_in[...] + ADAPTER_SCALE * mm(codes_mine_half, up_v[...])
    peak_s = jnp.max(student, axis=1, keepdims=True)
    sum_s = jnp.sum(jnp.exp(student - peak_s), axis=1, keepdims=True)
    cross = jnp.sum(exp_t * (tl - student), axis=1, keepdims=True)

    lane = lax.broadcasted_iota(jnp.int32, (half, 128), 1)
    packed = jnp.zeros((half, 128), F32)
    for i, value in enumerate((peak_s, sum_s, peak_t, sum_t, cross)):
        packed = jnp.where(lane == i, value, packed)
    stats[...] = packed.T[:8, :]
    stat_sends = []
    for k in range(1, peers):
        stat_sends.append(remote(stats, stats_in.at[me], st_s.at[k], st_r.at[k], peer(k)[1]))
        stat_sends[-1].start()
    stats_in[me] = stats[...]
    code_rest.wait_recv()
    codes_t[...] = (codes_mine[...].astype(F32) + codes_other[...].astype(F32)).T.astype(BF16)
    for copy in stat_sends:
        copy.wait_recv()
    got = [stats_in[i] for i in range(peers)]
    top_s, top_t = got[0][0:1], got[0][2:3]
    for one in got[1:]:
        top_s, top_t = jnp.maximum(top_s, one[0:1]), jnp.maximum(top_t, one[2:3])
    zs_sum = zt_sum = cross_sum = jnp.zeros_like(top_s)
    for one in got:
        zs_sum = zs_sum + one[1:2] * jnp.exp(one[0:1] - top_s)
        scale = jnp.exp(one[2:3] - top_t)
        zt_sum = zt_sum + one[3:4] * scale
        cross_sum = cross_sum + one[4:5] * scale
    log_zs = top_s + jnp.log(zs_sum)
    log_zt = top_t + jnp.log(zt_sum)
    kl_out[...] = cross_sum / zt_sum - log_zt + log_zs
    flip[...] = jnp.zeros_like(flip)
    flip[0:1, :] = log_zs
    flip[1:2, :] = log_zt
    flip[2:3, :] = counted[...].astype(F32) / rows
    cols = flip[...].T
    grad_half = (cols[:, 2:3] * (jnp.exp(student - cols[:, 0:1]) - jnp.exp(tl - cols[:, 1:2]))).astype(BF16)
    vh = vocab_size // 2
    my_blocks = pl.ds(p * vh, vh)
    grad[my_blocks] = grad_half.reshape(vh, token_size, block, columns)
    grad_pair = remote(grad.at[my_blocks], grad.at[my_blocks], pair_s.at[2], pair_r.at[2], mate)
    grad_pair.start()
    down_tok.wait_recv()
    arrived = d_all.at[pl.ds(pl.multiple_of((1 - t) * rank + v * share, share), share)]
    down_sends = []
    for k in range(1, vocab_size):
        down_sends.append(remote(arrived, arrived, dn_s.at[k], dn_r.at[k], {"vocab": lax.rem(v + k, vocab_size)}))
        down_sends[-1].start()
    grad_pair.wait_recv()

    group = vocab_size * block
    g_other = grad[:, 1 - t].reshape(group, columns)
    x_sends = []
    for j in range(PARTS):
        xs[j] = mm(g_other, w[pl.ds(j * part, part), :], NT).astype(BF16).reshape(vocab_size, block, part)
        x_sends.append(remote(xs.at[j], xr.at[j], xs_s.at[j], xs_r.at[j], across))
        x_sends[-1].start()
        if j == 0:
            g_all = grad[...].reshape(rows, columns)
            cgp[...] = (mm(g_all, up_v[...], NT) * mask[...]).astype(BF16).reshape(peers, block, rank2)
            cp_sends = []
            for k in range(1, peers):
                b, where = peer(k)
                cp_sends.append(remote(cgp.at[b], cgp_in.at[me], cp_s.at[k], cp_r.at[k], where))
                cp_sends[-1].start()
            cgp_in[me] = cgp[me]
    g_own = grad[:, t].reshape(group, columns)
    for j in range(PARTS):
        own[j] = mm(g_own, w[pl.ds(j * part, part), :], NT).reshape(vocab_size, block, part)

    up_out[...] = (ADAPTER_SCALE * mm(codes_t[...], g_all)).astype(BF16)

    z_sends = []
    for j in range(PARTS):
        if j == PARTS // 2:
            for copy in cp_sends:
                copy.wait_recv()
            total = cgp_in[0].astype(F32)
            for i in range(1, peers):
                total = total + cgp_in[i].astype(F32)
            cg_all[me] = total.astype(BF16)
            cg_sends = []
            for k in range(1, peers):
                cg_sends.append(remote(cg_all.at[me], cg_all.at[me], cg_s.at[k], cg_r.at[k], peer(k)[1]))
                cg_sends[-1].start()
        x_sends[j].wait_recv()
        merged = own[j] + xr[j].astype(F32)
        own[j] = merged
        zs[j] = merged.astype(BF16)
        for k in range(1, vocab_size):
            to = lax.rem(v + k, vocab_size)
            z_sends.append(remote(zs.at[j, to], zr.at[j, k], z_s.at[j, k], z_r.at[j, k], {"vocab": to}))
            z_sends[-1].start()
    for copy in cg_sends:
        copy.wait_recv()
    cg_t[...] = cg_all[...].reshape(rows, rank2).astype(F32).T.astype(BF16)
    down_out[...] = (ADAPTER_SCALE * mm(cg_t[at_rows(t, rank), :], h[...])).astype(BF16)

    for copy in down_sends:
        copy.wait_recv()
    my_cg = cg_all[me]
    for j in range(PARTS):
        for k in range(1, vocab_size):
            z_sends[j * (vocab_size - 1) + k - 1].wait_recv()
        value = own[j, v] + ADAPTER_SCALE * mm(my_cg, d_all[:, pl.ds(j * part, part)])
        for k in range(1, vocab_size):
            value = value + zr[j, k].astype(F32)
        hidden_out[:, pl.ds(j * part, part)] = value.astype(BF16)

    for copy in [code_pair, logit_pair, logit_last, grad_pair, code_tok, code_rest, down_tok] + sends + forwards + down_sends + stat_sends + cp_sends + cg_sends + x_sends + z_sends:
        copy.wait_send()


def hand_over(*refs):
    sources, targets, held, sem_in, sem_out = refs[:4], refs[4:8], refs[8:12], refs[12], refs[13]
    reads = [pltpu.make_async_copy(sources[i], held[i], sem_in.at[i]) for i in range(4)]
    writes = [pltpu.make_async_copy(held[i], targets[i], sem_out.at[i]) for i in range(4)]
    for read in reads:
        read.start()
    for read, write in zip(reads, writes):
        read.wait()
        write.start()
    for write in writes:
        write.wait()


def fused_shards(hidden, student_head_weight, down_weight, up_weight, teacher, tenant, counted_row_mask):
    vocab_size, token_size = lax.axis_size("vocab"), lax.axis_size("tokens")
    peers = vocab_size * token_size
    rows = tenant.shape[0]
    half = rows // 2
    block = rows // peers
    width, columns = student_head_weight.shape
    tenants, rank, _ = up_weight.shape
    rank2 = tenants * rank
    part = width // PARTS
    down_t = jnp.swapaxes(down_weight[0], 0, 1)
    vmem = pl.BlockSpec(memory_space=pltpu.VMEM)
    hbm = pl.BlockSpec(memory_space=pl.ANY)
    dma = pltpu.SemaphoreType.DMA
    kernel = functools.partial(fused, vocab_size, token_size)
    token_kl, hidden_gradient, down_gradient, up_gradient = pl.pallas_call(
        kernel,
        out_shape=(
            jax.ShapeDtypeStruct((1, half), F32),
            jax.ShapeDtypeStruct((block, width), BF16),
            jax.ShapeDtypeStruct((rank, width), BF16),
            jax.ShapeDtypeStruct((rank2, columns), BF16),
        ),
        in_specs=[hbm] * 5 + [vmem] * 2,
        out_specs=(vmem,) * 4,
        scratch_shapes=[
            pltpu.VMEM((rows, rank2), F32),
            pltpu.VMEM((rows, width), BF16),
            pltpu.VMEM((width, columns), BF16),
            pltpu.VMEM((rank2, width), BF16),
            pltpu.VMEM((rank2, width), BF16),
            pltpu.VMEM((rank2, columns), BF16),
            pltpu.VMEM((half, columns), BF16),
            pltpu.VMEM((rows, columns), F32),
            pltpu.VMEM((half, columns), F32),
            pltpu.VMEM((rows, rank2), F32),
            pltpu.VMEM((rows, rank2), F32),
            pltpu.VMEM((rows, rank2), BF16),
            pltpu.VMEM((rows, rank2), BF16),
            pltpu.VMEM((rank2, rows), BF16),
            pltpu.VMEM((8, half), F32),
            pltpu.VMEM((peers, 8, half), F32),
            pltpu.VMEM((128, half), F32),
            pltpu.VMEM((vocab_size, token_size, block, columns), BF16),
            pltpu.VMEM((peers, block, rank2), BF16),
            pltpu.VMEM((peers, block, rank2), BF16),
            pltpu.VMEM((peers, block, rank2), BF16),
            pltpu.VMEM((rank2, rows), BF16),
            pltpu.VMEM((PARTS, vocab_size, block, part), BF16),
            pltpu.VMEM((PARTS, vocab_size, block, part), BF16),
            pltpu.VMEM((PARTS, vocab_size, block, part), F32),
            pltpu.VMEM((PARTS, vocab_size, block, part), BF16),
            pltpu.VMEM((PARTS, vocab_size, block, part), BF16),
            dma((7,)), dma((PIECES,)), dma((PIECES,)), dma((PIECES,)), dma((PIECES,)), dma((4,)), dma((4,)), dma((3,)), dma((3,)),
            dma((peers,)), dma((peers,)), dma((peers,)), dma((peers,)), dma((peers,)), dma((peers,)),
            dma((vocab_size,)), dma((vocab_size,)), dma((PARTS,)), dma((PARTS,)), dma((PARTS, vocab_size)), dma((PARTS, vocab_size)),
        ],
        compiler_params=pltpu.CompilerParams(
            collective_id=0, has_side_effects=True, vmem_limit_bytes=60 << 20
        ),
    )(hidden, student_head_weight, down_t, up_weight.reshape(rank2, columns), teacher, tenant.reshape(1, rows),
      counted_row_mask.reshape(1, half))
    made = (token_kl, hidden_gradient, down_gradient, up_gradient)
    token_kl, hidden_gradient, down_gradient, up_gradient = pl.pallas_call(
        hand_over,
        out_shape=tuple(jax.ShapeDtypeStruct(one.shape, one.dtype) for one in made),
        in_specs=[hbm] * 4,
        out_specs=(hbm,) * 4,
        scratch_shapes=[pltpu.VMEM(one.shape, one.dtype) for one in made] + [dma((4,)), dma((4,))],
        compiler_params=pltpu.CompilerParams(vmem_limit_bytes=60 << 20),
    )(*made)
    return (
        token_kl.reshape(half),
        hidden_gradient,
        jnp.swapaxes(down_gradient, 0, 1)[None],
        up_gradient.reshape(tenants, rank, columns),
    )


def fits(mesh):
    return mesh.shape["tokens"] == 2 and mesh.shape["vocab"] == 4


def solution(mesh):
    return jax.shard_map(
        fused_shards if fits(mesh) else shards,
        mesh=mesh,
        in_specs=(
            P(("groups", "tokens"), "pair"),
            P("pair", ("vocab", "tokens")),
            P("tokens", "pair", None),
            P(None, None, ("vocab", "tokens")),
            P(("groups", "pair"), ("vocab", "tokens")),
            P("groups"),
            P(("groups", "pair")),
        ),
        out_specs=(
            P(("groups", "pair")),
            P(("groups", "vocab", "tokens"), "pair"),
            P(("groups", "tokens"), "pair", None),
            P("groups", None, ("vocab", "tokens")),
        ),
        check_vma=False,
    )
```
